256 devices in a mesh: ctx: 16 (over x, y_lo, core), exp: 16 (over y_hi, z).
Axes of the slice: x: 4, y: 4 (y_hi: 2, y_lo: 2; y = y_hi * 2 + y_lo), z: 8, core: 2. Of those that a mesh axis runs over, the one named last changes fastest.
Arguments:
- queries: bfloat16 [16, 2048, 1024], P('exp', 'ctx'), may hold values from -40 to 40
- keys: bfloat16 [16, 2048, 1024], P('exp', 'ctx'), may hold values from -6 to 6
- values: bfloat16 [16, 2048, 1024], P('exp', 'ctx'), may hold values from -6 to 6
- segments: int32 [16, 2048], P('exp'), may hold values from 0 to 7, never falling along the last dimension, each value on 1 to 1152 neighbouring positions
- hidden_state: bfloat16 [16, 2048, 2048], P('exp', 'ctx'), may hold values from -40 to 40
- norm_gain: float32 [2048], replicated, may hold values from 0.1 to 1.9
- route_gates: float32 [16, 2048, 2], P('exp', 'ctx'), may hold values from 0.2 to 1
- routes: int32 [16, 2048, 2], P('exp', 'ctx'), may hold values from 0 to 15, all different within a row; in each aligned block of 128 rows (0 to 127, 128 to 255, ..., all dimensions but the last counted through in order) at most 24 rows name the same one
- out_grad: bfloat16 [16, 2048, 2048], P('exp', 'ctx'), may hold values from -6 to 6
- w_gate: bfloat16 [16, 2048, 512], P('exp'), may hold values from -0.125 to 0.125
- w_up: bfloat16 [16, 2048, 512], P('exp'), may hold values from -0.125 to 0.125
- w_down: bfloat16 [16, 512, 2048], P('exp'), may hold values from -0.25 to 0.25
Outputs:
- query_grad: bfloat16 [16, 2048, 1024], P('exp', 'ctx')
- key_grad: bfloat16 [16, 2048, 1024], P('exp', 'ctx')
- value_grad: bfloat16 [16, 2048, 1024], P('exp', 'ctx')
- residual_grad: bfloat16 [16, 2048, 2048], P('exp', 'ctx')
The draws below stay inside these ranges and needn't reach their ends.
Inputs may be any that keep to these rules, and one draw needn't show every extreme that they name: Among the frames of one device (aligned blocks of 128 frames) no expert is named by more than 24 routes, a bound that some block reaches; a frame names 2 different experts. `segments`: segment ids never fall along a sequence; a segment holds 1 to 1152 frames and one holds exactly 1152.
All inputs are finite; a program needn't handle non-finite values.
Results may differ from the reference program's by a relative error of at most 0.015.
Values may be sent and summed in bfloat16 or wider, within the bound.
No kernel may reach another device: no remote copies, remote signals or barrier semaphores. Data moves between devices by JAX's collectives and lax.ppermute only.
A program may use at most 128 MiB of HBM per device.

```python
import math
import jax
import jax.numpy as jnp
import numpy as np
from jax import lax

D = 2048
HEADS = 8
HEAD_DIM = 128
FF = 512
TOP = 2
SEG_COUNT = 8
TOK_DEV = 128
ATT_WIDTH = 1024
LENGTH = 2048
BATCH = 16
EXPERTS = 16
CAP = 24
SEG_MOST = 1152
N_CTX = 16
N_EXP = 16


def draw_keys(key, part):
    key = jax.random.fold_in(key, 2)
    drawn = jax.random.normal(key, (BATCH, LENGTH, ATT_WIDTH), jnp.float32)
    return jnp.clip(drawn, -6.0, 6.0).astype(jnp.bfloat16)


def draw_queries(key, part):
    key = jax.random.fold_in(key, 1)
    drawn = jax.random.normal(key, (BATCH, LENGTH, ATT_WIDTH), jnp.float32)
    return jnp.clip(drawn, -40.0, 40.0).astype(jnp.bfloat16)


def draw_hidden_state(key, part):
    key = jax.random.fold_in(key, 3)
    first, second, third = jax.random.split(key, 3)
    row_scale = jnp.exp(jax.random.uniform(second, (BATCH, LENGTH, 1), jnp.float32, -1.15, 1.15))
    col_scale = jnp.exp(jax.random.uniform(third, (1, 1, D), jnp.float32, -1.15, 1.15))
    drawn = jnp.clip(jax.random.normal(first, (BATCH, LENGTH, D), jnp.float32), -4.0, 4.0)
    return jnp.clip(drawn * row_scale * col_scale, -40.0, 40.0).astype(jnp.bfloat16)


def steps_of(key, shape, pieces, low, top_value):
    level = 1.0
    for axis_at, blocks in pieces:
        steps = jax.random.uniform(jax.random.fold_in(jax.random.fold_in(key, 6), axis_at), (blocks,), jnp.float32, low / len(pieces), top_value / len(pieces))
        level = level * jnp.repeat(jnp.exp(steps), shape[axis_at] // blocks).reshape((-1,) + (1,) * (len(shape) - 1 - axis_at))
    return level


def profile(number_of, total, most, skew):
    weights = [(1 << 20) // math.isqrt(rank ** skew) + 1 for rank in range(2, number_of + 1)]
    rest, given = total - most - (number_of - 1), [1] * (number_of - 1)
    while rest > 0:
        movable = [i for i in range(number_of - 1) if given[i] < most]
        pool, budget = sum([weights[i] for i in movable]), rest
        for i in movable:
            extra = min(most - given[i], max(1, budget * weights[i] // pool), rest)
            given[i] = given[i] + extra
            rest = rest - extra
    return np.array([most] + given)


def uneven(key, number_of, total, reach, lean):
    if number_of == 2:
        one = jax.random.randint(key, (), max(1, total - reach), min(reach, total - 1) + 1)
        return jnp.stack([one, total - one])
    sizes = jnp.asarray(profile(number_of, total, reach, lean), jnp.int32)
    pairs = (number_of - 1) // 2
    donor, taker = sizes[1:1 + 2 * pairs:2], sizes[2:2 + 2 * pairs:2]
    margin = jnp.minimum(donor - 1, reach - taker)
    moved = jax.random.randint(jax.random.fold_in(key, 1), (pairs,), 0, 1 << 20) % (margin + 1)
    sizes = sizes.at[1:1 + 2 * pairs:2].set(donor - moved).at[2:2 + 2 * pairs:2].set(taker + moved)
    return sizes[jax.random.permutation(jax.random.fold_in(key, 2), number_of)]


def routed_block(own_key, own, number, rows, count, top, most, skew):
    ranking = jax.random.permutation(own_key, count)
    crowded, usual = load_shares(count, rows * top, most, skew, True), load_shares(count, rows * top, most, skew, False)
    places = jnp.arange(count)

    def named(sizes, offset_by):
        used = int((sizes > 0).sum())
        fixed = max(1, used // 4)
        passed = fixed + (places - fixed + offset_by * (used - fixed)) % max(1, count - fixed)
        return jnp.zeros((count,), jnp.int32).at[ranking[jnp.where(places < fixed, places, passed)]].set(jnp.asarray(sizes, jnp.int32))

    sizes = jnp.where(number % 4 == 0, named(crowded, number // 4), named(usual, number - number // 4 - 1))
    mixed = jax.random.permutation(jax.random.fold_in(own, 3), count)
    giver, sink = mixed[0:count // 2 * 2:2], mixed[1:count // 2 * 2:2]
    slack = jnp.minimum(sizes[giver] - 1, most - sizes[sink]) // 2
    slack = jnp.where((giver == ranking[0]) | (sink == ranking[0]) | (sizes[sink] == 0), 0, jnp.maximum(slack, 0))
    passed = jax.random.randint(jax.random.fold_in(own, 4), (count // 2,), 0, 1 << 20) % (slack + 1)
    sizes = sizes.at[giver].add(-passed).at[sink].add(passed)
    items = jnp.searchsorted(jnp.cumsum(sizes), jnp.arange(rows * top), side="right").astype(jnp.int32)
    grid = items.reshape(top, rows).T
    grid = grid[jax.random.permutation(jax.random.fold_in(own, 1), rows)]
    offset_by = jax.random.randint(jax.random.fold_in(own, 2), (rows, 1), 0, top)
    return jnp.take_along_axis(grid, (jnp.arange(top)[None, :] + offset_by) % top, axis=1)


def load_shares(number_of, total, reach, lean, full):
    weights = [(1 << 20) // math.isqrt(grade ** lean) + 1 for grade in range(1, number_of + 1)]
    largest = reach if full else min(reach, max(-(-total // number_of), total * weights[0] // sum(weights)))
    least = 1 if total - largest >= number_of - 1 else 0
    holding, spare = [largest] + [least] * (number_of - 1), total - largest - least * (number_of - 1)
    while spare > 0:
        free = [i for i in range(1, number_of) if holding[i] < largest] or [i for i in range(1, number_of) if holding[i] < reach]
        mass, remaining = sum([weights[i] for i in free]), spare
        for i in free:
            extra = min(reach - holding[i], max(1, remaining * weights[i] // mass), spare)
            holding[i] = holding[i] + extra
            spare = spare - extra
    return np.array(holding)


def noise(key, shape, scale, reach, shards=(), kind=jnp.bfloat16):
    factor_of = steps_of(key, shape, shards, -0.22, 0.18) if shards else 1.0
    array = jax.random.normal(key, shape, jnp.float32) * scale * factor_of
    return jnp.minimum(jnp.maximum(array, -reach), reach).astype(kind)


def setup_inputs(seed: int = 0) -> dict:
    key_list = jax.random.split(jax.random.key(seed), 13)
    queries = draw_queries(jax.random.fold_in(key_list[12], 71), 0)
    keys = draw_keys(jax.random.fold_in(key_list[12], 71), 0)
    values = noise(key_list[2], (BATCH, LENGTH, ATT_WIDTH), 1.0, 6.0, ((0, 16), (1, 16)))
    segments = jax.vmap(lambda own: jnp.searchsorted(jnp.cumsum(uneven(own, SEG_COUNT, LENGTH, SEG_MOST, 2)), jnp.arange(LENGTH), side="right"))(jax.random.split(key_list[3], BATCH)).reshape((BATCH, LENGTH)).astype(jnp.int32)
    hidden_state = draw_hidden_state(jax.random.fold_in(key_list[12], 71), 0)
    norm_gain = jnp.clip(1.0 + 0.18 * jax.random.normal(key_list[5], (D,), jnp.float32), 0.1, 1.9)
    route_gates = jnp.clip(0.2 + 0.8 * jax.random.uniform(key_list[6], (BATCH, LENGTH, TOP), jnp.float32) ** steps_of(key_list[6], (BATCH, LENGTH, TOP), ((0, 16), (1, 16)), -0.2, 0.2), 0.2, 1.0)
    routes_keys = jax.random.split(jax.random.fold_in(key_list[7], 1), BATCH * LENGTH // TOK_DEV)
    routes_turns = jax.random.permutation(jax.random.fold_in(key_list[7], 3), BATCH * LENGTH // TOK_DEV)
    routes = jax.vmap(lambda own, number: routed_block(jax.random.fold_in(key_list[7], 2), own, number, TOK_DEV, EXPERTS, TOP, CAP, 1))(routes_keys, routes_turns).reshape((BATCH, LENGTH, TOP))
    out_grad = noise(key_list[8], (BATCH, LENGTH, D), 1.0, 6.0, ((0, 16), (1, 16)))
    w_gate = noise(key_list[9], (EXPERTS, D, FF), D ** -0.5, 0.125, ((0, 16),))
    w_up = noise(key_list[10], (EXPERTS, D, FF), D ** -0.5, 0.125, ((0, 16),))
    w_down = noise(key_list[11], (EXPERTS, FF, D), FF ** -0.5, 0.25, ((0, 16),))
    return dict(queries=queries, keys=keys, values=values, segments=segments, hidden_state=hidden_state, norm_gain=norm_gain, route_gates=route_gates, routes=routes, out_grad=out_grad, w_gate=w_gate, w_up=w_up, w_down=w_down)


EPSILON = 1e-06
MASKED = -1e+30

def silu_parts(pre_act):
    sigmoid = jax.nn.sigmoid(pre_act)
    return (pre_act * sigmoid, sigmoid * (1.0 + pre_act * (1.0 - sigmoid)))

def expert_backward(normed_rows, scaled_rows, gate_mat, up_mat, down_mat):
    contract = (((1,), (1,)), ((), ()))
    gate_pre = jnp.dot(normed_rows, gate_mat, preferred_element_type=jnp.float32)
    up_pre = jnp.dot(normed_rows, up_mat, preferred_element_type=jnp.float32)
    hidden_grad = lax.dot_general(scaled_rows, down_mat, contract, preferred_element_type=jnp.float32)
    activated, slope = silu_parts(gate_pre)
    gate_grad = (hidden_grad * up_pre * slope).astype(jnp.bfloat16)
    up_grad = (hidden_grad * activated).astype(jnp.bfloat16)
    summed = lax.dot_general(gate_grad, gate_mat, contract, preferred_element_type=jnp.float32)
    summed = summed + lax.dot_general(up_grad, up_mat, contract, preferred_element_type=jnp.float32)
    return summed.astype(jnp.bfloat16)

def reference(queries, keys, values, segments, hidden_state, norm_gain, route_gates, routes, out_grad, w_gate, w_up, w_down):
    frames = BATCH * LENGTH
    hidden_f = hidden_state.astype(jnp.float32)
    inverse = lax.rsqrt(lax.optimization_barrier(jnp.mean(hidden_f * hidden_f, -1, keepdims=True)) + EPSILON)
    normed = (hidden_f * inverse * norm_gain).astype(jnp.bfloat16)
    scaled = (route_gates[..., None] * out_grad[:, :, None, :].astype(jnp.float32)).astype(jnp.bfloat16)
    flat_normed = jnp.concatenate([normed.reshape(frames, D), jnp.zeros((1, D), jnp.bfloat16)], 0)
    flat_scaled = jnp.concatenate([scaled.reshape(frames * TOP, D), jnp.zeros((1, D), jnp.bfloat16)], 0)
    chosen = routes.reshape(frames * TOP)
    row_count = N_EXP * N_CTX * CAP

    def per_expert(running, inputs):
        gate_mat, up_mat, down_mat, index = inputs
        picked = jnp.nonzero(chosen == index, size=row_count, fill_value=frames * TOP)[0]
        frame_of = picked // TOP
        back = expert_backward(flat_normed[frame_of], flat_scaled[picked], gate_mat, up_mat, down_mat)
        running = running.at[frame_of].add(back.astype(jnp.float32), mode='drop')
        return (running, None)
    normed_grad, unused = lax.scan(per_expert, jnp.zeros((frames, D), jnp.float32), (w_gate, w_up, w_down, jnp.arange(EXPERTS, dtype=jnp.int32)))
    weighted = norm_gain * normed_grad.reshape(BATCH, LENGTH, D)
    residual = out_grad.astype(jnp.float32) + inverse * weighted
    residual = residual - hidden_f * inverse ** 3 * lax.optimization_barrier(jnp.mean(hidden_f * weighted, -1, keepdims=True))
    residual_grad = residual.astype(jnp.bfloat16)
    inv_root = HEAD_DIM ** (-0.5)
    highest = lax.Precision.HIGHEST

    def one_sequence(inputs):
        query_in, key_in, value_in, seg_ids, resid = inputs
        query_f = query_in.reshape(LENGTH, HEADS, HEAD_DIM).astype(jnp.float32)
        key_f = key_in.reshape(LENGTH, HEADS, HEAD_DIM).astype(jnp.float32)
        value_f = value_in.reshape(LENGTH, HEADS, HEAD_DIM).astype(jnp.float32)
        grad_out = resid[:, :ATT_WIDTH].reshape(LENGTH, HEADS, HEAD_DIM).astype(jnp.float32)
        allowed = (seg_ids[:, None] == seg_ids[None, :])[None]
        scores = jnp.einsum('qhd,khd->hqk', query_f, key_f, precision=highest) * inv_root
        scores = jnp.where(allowed, scores, MASKED)
        row_peak = lax.optimization_barrier(jnp.max(scores, -1))
        summed = lax.optimization_barrier(jnp.sum(jnp.where(allowed, jnp.exp(scores - row_peak[..., None]), 0.0), -1))
        lse = row_peak + jnp.log(summed)
        attend = jnp.where(allowed, jnp.exp(scores - lse[..., None]), 0.0)
        out = jnp.einsum('hqk,khd->hqd', attend, value_f, precision=highest)
        delta = lax.optimization_barrier(jnp.sum(jnp.transpose(grad_out, (1, 0, 2)) * out, -1))
        attend_b = attend.astype(jnp.bfloat16).astype(jnp.float32)
        value_grad = jnp.einsum('hqk,qhd->khd', attend_b, grad_out, precision=highest)
        attend_grad = jnp.einsum('qhd,khd->hqk', grad_out, value_f, precision=highest)
        score_grad = (attend * (attend_grad - delta[..., None])).astype(jnp.bfloat16).astype(jnp.float32)
        key_grad = jnp.einsum('hqk,qhd->khd', score_grad, query_f, precision=highest) * inv_root
        query_grad = jnp.einsum('hqk,khd->qhd', score_grad, key_f, precision=highest) * inv_root
        return (query_grad.reshape(LENGTH, ATT_WIDTH).astype(jnp.bfloat16), key_grad.reshape(LENGTH, ATT_WIDTH).astype(jnp.bfloat16), value_grad.reshape(LENGTH, ATT_WIDTH).astype(jnp.bfloat16))
    query_grad, key_grad, value_grad = lax.map(one_sequence, (queries, keys, values, segments, residual_grad))
    return (query_grad, key_grad, value_grad, residual_grad)
```

```python
import functools

import jax
import jax.numpy as jnp
from jax import lax
from jax.experimental import pallas as pl
from jax.experimental.pallas import tpu as pltpu
from jax.sharding import PartitionSpec as P

HEAD_DIM = 128
TOP = 2
EPSILON = 1e-06
MASKED = -1e30
LANES = 128
NT = (((1,), (1,)), ((), ()))
MIB = 1 << 20
VMEM = pltpu.MemorySpace.VMEM


def params(limit_mib, **more):
    return pltpu.CompilerParams(vmem_limit_bytes=limit_mib * MIB, **more)


def dot(a, b):
    return jnp.dot(a, b, preferred_element_type=jnp.float32)


def dot_nt(a, b):
    return lax.dot_general(a, b, NT, preferred_element_type=jnp.float32)


def three_parts(x):
    high = x.astype(jnp.bfloat16)
    rest = x - high.astype(jnp.float32)
    mid = rest.astype(jnp.bfloat16)
    low = (rest - mid.astype(jnp.float32)).astype(jnp.bfloat16)
    return high, mid, low


def pack_kernel(
    n_exp, capacity, steps, width,
    routes_ref, gates_ref, hidden_ref, gain_ref, out_grad_ref,
    send_ref, back_ref, inverse_ref,
    normed_scr, pick_scr, gate_scr,
):
    step = pl.program_id(0)
    rows = hidden_ref.shape[0]
    slots = n_exp * capacity

    @pl.when(step == 0)
    def _():
        hidden = hidden_ref[...].astype(jnp.float32)
        inverse = lax.rsqrt(jnp.mean(hidden * hidden, -1, keepdims=True) + EPSILON)
        normed_scr[...] = (hidden * inverse * gain_ref[...]).astype(jnp.bfloat16)
        inverse_ref[...] = jnp.broadcast_to(inverse, inverse_ref.shape)
        expert_id = lax.broadcasted_iota(jnp.int32, (n_exp, rows), 0)
        earlier = (
            lax.broadcasted_iota(jnp.int32, (rows, rows), 0)
            < lax.broadcasted_iota(jnp.int32, (rows, rows), 1)
        ).astype(jnp.bfloat16)
        slot_id = lax.broadcasted_iota(jnp.int32, (slots, rows), 0).astype(jnp.float32)
        first_slot = expert_id.astype(jnp.float32) * capacity
        total = None
        for j in range(TOP):
            named = (expert_id == routes_ref[j : j + 1, :]).astype(jnp.float32)
            place = first_slot + dot(named.astype(jnp.bfloat16), earlier)
            if j:
                place = place + used
            target = jnp.sum(named * place, 0, keepdims=True)
            pick = (slot_id == target).astype(jnp.float32)
            pick_scr[:, j * rows : (j + 1) * rows] = pick.astype(jnp.bfloat16)
            total = pick if total is None else total + pick
            if j == 0:
                used = jnp.sum(named, 1, keepdims=True)
            gate_scr[j] = jnp.broadcast_to(gates_ref[j : j + 1, :], (rows, rows)).T
        back_ref[...] = total.T.astype(jnp.bfloat16)

    @pl.when(step < steps)
    def _():
        columns = pl.ds(pl.multiple_of(step * width, width), width)
        part = normed_scr[:, columns]
        both = jnp.concatenate([part, part], 0)
        send_ref[...] = dot(pick_scr[...], both).astype(jnp.bfloat16)

    @pl.when(step >= steps)
    def _():
        columns = pl.ds(pl.multiple_of((step - steps) * width, width), width)
        part = out_grad_ref[:, columns].astype(jnp.float32)
        both = jnp.concatenate(
            [(gate_scr[j][:, :1] * part).astype(jnp.bfloat16) for j in range(TOP)], 0
        )
        send_ref[...] = dot(pick_scr[...], both).astype(jnp.bfloat16)


def pack(routes_t, gates_t, hidden, gain, out_grad, n_exp, capacity):
    rows, model = hidden.shape
    slots = n_exp * capacity
    width = 512
    steps = model // width
    whole = lambda shape: pl.BlockSpec(shape, lambda i: (0,) * len(shape))
    return pl.pallas_call(
        functools.partial(pack_kernel, n_exp, capacity, steps, width),
        grid=(2 * steps,),
        in_specs=[
            whole((TOP, rows)),
            whole((TOP, rows)),
            whole((rows, model)),
            whole((1, model)),
            whole((rows, model)),
        ],
        out_specs=[
            pl.BlockSpec((slots, width), lambda i: (0, i)),
            whole((rows, slots)),
            whole((rows, LANES)),
        ],
        out_shape=[
            jax.ShapeDtypeStruct((slots, 2 * model), jnp.bfloat16),
            jax.ShapeDtypeStruct((rows, slots), jnp.bfloat16),
            jax.ShapeDtypeStruct((rows, LANES), jnp.float32),
        ],
        scratch_shapes=[
            pltpu.VMEM((rows, model), jnp.bfloat16),
            pltpu.VMEM((slots, TOP * rows), jnp.bfloat16),
            pltpu.VMEM((TOP, rows, rows), jnp.float32),
        ],
        compiler_params=params(40),
        cost_estimate=pl.CostEstimate(
            flops=2 * slots * 4 * rows * model, bytes_accessed=8 * slots * model, transcendentals=0
        ),
        name="pack_rows",
    )(routes_t, gates_t, hidden, gain, out_grad)


def expert_kernel(
    model, front,
    rows_ref, gate_ref, up_ref, down_ref,
    front_ref, gate_grad_ref, up_grad_ref,
    total_scr, along_scr,
):
    step = pl.program_id(0)
    normed = rows_ref[:, :model]
    scaled = rows_ref[:, model:]
    gate_pre = dot(normed, gate_ref[...])
    up_pre = dot(normed, up_ref[...])
    hidden_grad = dot_nt(scaled, down_ref[...])
    sigmoid = jax.nn.sigmoid(gate_pre)
    slope = sigmoid * (1.0 + gate_pre * (1.0 - sigmoid))
    gate_grad = (hidden_grad * up_pre * slope).astype(jnp.bfloat16)
    up_grad = (hidden_grad * gate_pre * sigmoid).astype(jnp.bfloat16)
    gate_grad_ref[...] = gate_grad
    up_grad_ref[...] = up_grad
    along = jnp.sum(
        gate_grad.astype(jnp.float32) * gate_pre + up_grad.astype(jnp.float32) * up_pre,
        -1,
        keepdims=True,
    )
    part = dot_nt(gate_grad, gate_ref[:front, :]) + dot_nt(up_grad, up_ref[:front, :])

    @pl.when(step == 0)
    def _():
        total_scr[...] = part
        along_scr[...] = jnp.broadcast_to(along, along_scr.shape)

    @pl.when(step > 0)
    def _():
        total_scr[...] += part
        along_scr[...] += jnp.broadcast_to(along, along_scr.shape)

    @pl.when(step == pl.num_programs(0) - 1)
    def _():
        front_ref[:, :front] = total_scr[...].astype(jnp.bfloat16)
        whole = along_scr[...]
        high = whole.astype(jnp.bfloat16).astype(jnp.float32)
        lane = lax.broadcasted_iota(jnp.int32, whole.shape, 1)
        tail = jnp.where(lane == 0, high, jnp.where(lane == 1, whole - high, 0.0))
        front_ref[:, front:] = tail.astype(jnp.bfloat16)


def expert(rows, gate_mat, up_mat, down_mat, front):
    slots = rows.shape[0]
    model, units = gate_mat.shape
    chunk = 256
    return pl.pallas_call(
        functools.partial(expert_kernel, model, front),
        grid=(units // chunk,),
        in_specs=[
            pl.BlockSpec((slots, 2 * model), lambda i: (0, 0)),
            pl.BlockSpec((model, chunk), lambda i: (0, i)),
            pl.BlockSpec((model, chunk), lambda i: (0, i)),
            pl.BlockSpec((chunk, model), lambda i: (i, 0)),
        ],
        out_specs=[
            pl.BlockSpec((slots, front + LANES), lambda i: (0, 0)),
            pl.BlockSpec((slots, chunk), lambda i: (0, i)),
            pl.BlockSpec((slots, chunk), lambda i: (0, i)),
        ],
        out_shape=[
            jax.ShapeDtypeStruct((slots, front + LANES), jnp.bfloat16),
            jax.ShapeDtypeStruct((slots, units), jnp.bfloat16),
            jax.ShapeDtypeStruct((slots, units), jnp.bfloat16),
        ],
        scratch_shapes=[
            pltpu.VMEM((slots, front), jnp.float32),
            pltpu.VMEM((slots, LANES), jnp.float32),
        ],
        compiler_params=params(40),
        cost_estimate=pl.CostEstimate(
            flops=2 * slots * units * (3 * model + 2 * front),
            bytes_accessed=6 * model * units + 4 * slots * model,
            transcendentals=slots * units,
        ),
        name="expert_rows",
    )(rows, gate_mat, up_mat, down_mat)


def attend_kernel(
    scale, query_ref, key_ref, value_ref, here_ref, all_ref, out_ref, column_ref, row_ref
):
    count = key_ref.shape[0] * key_ref.shape[1]
    key = key_ref[...].reshape(count, HEAD_DIM)
    value = value_ref[...].reshape(count, HEAD_DIM)
    allowed = here_ref[:, :1] == all_ref[...]
    scores = jnp.where(allowed, dot_nt(query_ref[...], key) * scale, MASKED)
    peak = jnp.max(scores, -1, keepdims=True)
    attend = jnp.where(allowed, jnp.exp(scores - peak), 0.0)
    summed = jnp.sum(attend, -1, keepdims=True)
    out_ref[...] = dot(attend.astype(jnp.bfloat16), value) / summed
    lse = jnp.broadcast_to(peak + jnp.log(summed), column_ref.shape)
    column_ref[...] = lse
    row_ref[...] = lse.T[:8, :]


def attend_own(query, gathered, here, every, heads):
    rows = query.shape[0]
    n_ctx = gathered.shape[0]
    count = n_ctx * rows
    own = pl.BlockSpec((rows, HEAD_DIM), lambda h: (0, h))
    return pl.pallas_call(
        functools.partial(attend_kernel, HEAD_DIM ** (-0.5)),
        grid=(heads,),
        in_specs=[
            own,
            pl.BlockSpec((n_ctx, None, rows, HEAD_DIM), lambda h: (0, 0, 0, h)),
            pl.BlockSpec((n_ctx, None, rows, HEAD_DIM), lambda h: (0, 1, 0, h)),
            pl.BlockSpec((rows, LANES), lambda h: (0, 0)),
            pl.BlockSpec((1, count), lambda h: (0, 0)),
        ],
        out_specs=[own, own, pl.BlockSpec((None, 8, rows), lambda h: (h, 0, 0))],
        out_shape=[
            jax.ShapeDtypeStruct((rows, heads * HEAD_DIM), jnp.float32),
            jax.ShapeDtypeStruct((rows, heads * HEAD_DIM), jnp.float32),
            jax.ShapeDtypeStruct((heads, 8, rows), jnp.float32),
        ],
        compiler_params=params(40),
        cost_estimate=pl.CostEstimate(
            flops=4 * rows * count * heads * HEAD_DIM,
            bytes_accessed=4 * count * heads * HEAD_DIM,
            transcendentals=rows * count * heads,
        ),
        name="attend_own",
    )(query, gathered, gathered, here, every)


def front_kernel(
    model, heads,
    returned_ref, back_ref, hidden_ref, out_grad_ref, gain_ref, inverse_ref, out_ref, lse_ref,
    grad_ref, delta_ref, along_ref,
):
    front = heads * HEAD_DIM
    rows = hidden_ref.shape[0]
    inverse = inverse_ref[:, :1]
    sums = dot(back_ref[...], returned_ref[...])
    along = jnp.sum(sums[:, front:], -1, keepdims=True) * (1.0 / model)
    along_ref[...] = jnp.broadcast_to(along, along_ref.shape)
    weighted = gain_ref[...] * sums[:, :front]
    hidden = hidden_ref[...].astype(jnp.float32)
    residual = out_grad_ref[...].astype(jnp.float32) + inverse * weighted
    residual = residual - hidden * (inverse * inverse * along)
    grad = residual.astype(jnp.bfloat16)
    grad_ref[:rows, :] = grad
    product = grad.astype(jnp.float32) * out_ref[...]
    pad = jnp.zeros((grad_ref.shape[0] - rows - 6, rows), jnp.bfloat16)
    for h in range(heads):
        columns = slice(h * HEAD_DIM, (h + 1) * HEAD_DIM)
        delta = jnp.broadcast_to(jnp.sum(product[:, columns], -1, keepdims=True), (rows, rows))
        delta_ref[:, columns] = delta
        parts = three_parts(delta.T[:1, :]) + three_parts(lse_ref[h][:1, :])
        parts = [part.astype(jnp.float32) for part in parts] + [pad.astype(jnp.float32)]
        grad_ref[rows:, columns] = jnp.concatenate(parts, 0).astype(jnp.bfloat16)


def front_grad(returned, back, hidden, out_grad, gain, inverse, out, lse_rows, heads):
    rows, model = hidden.shape
    slots = back.shape[1]
    front = heads * HEAD_DIM
    extra = 16
    whole = lambda shape: pl.BlockSpec(shape, lambda i: (0,) * len(shape))
    return pl.pallas_call(
        functools.partial(front_kernel, model, heads),
        grid=(1,),
        in_specs=[
            whole((slots, front + LANES)),
            whole((rows, slots)),
            whole((rows, front)),
            whole((rows, front)),
            whole((1, front)),
            whole((rows, LANES)),
            whole((rows, front)),
            whole((heads, 8, rows)),
        ],
        out_specs=[whole((rows + extra, front)), whole((rows, front)), whole((rows, LANES))],
        out_shape=[
            jax.ShapeDtypeStruct((rows + extra, front), jnp.bfloat16),
            jax.ShapeDtypeStruct((rows, front), jnp.float32),
            jax.ShapeDtypeStruct((rows, LANES), jnp.float32),
        ],
        compiler_params=params(40),
        cost_estimate=pl.CostEstimate(
            flops=2 * slots * rows * front, bytes_accessed=6 * slots * front, transcendentals=0
        ),
        name="front_grad",
    )(returned, back, hidden, out_grad, gain, inverse, out, lse_rows)


def rest_kernel(
    front, returned_ref, back_ref, hidden_ref, out_grad_ref, gain_ref, inverse_ref, along_ref,
    grad_ref, residual_ref,
):
    rows = hidden_ref.shape[0]
    inverse = inverse_ref[:, :1]
    weighted = gain_ref[:, front:] * dot(back_ref[...], returned_ref[...])
    hidden = hidden_ref[:, front:].astype(jnp.float32)
    residual = out_grad_ref[:, front:].astype(jnp.float32) + inverse * weighted
    residual = residual - hidden * (inverse * inverse * along_ref[:, :1])
    residual_ref[:, front:] = residual.astype(jnp.bfloat16)
    residual_ref[:, :front] = grad_ref[:rows, :]


def rest_grad(returned, back, hidden, out_grad, gain, inverse, along, grad):
    rows, model = hidden.shape
    front = grad.shape[1]
    return pl.pallas_call(
        functools.partial(rest_kernel, front),
        out_shape=jax.ShapeDtypeStruct((rows, model), jnp.bfloat16),
        compiler_params=params(40),
        cost_estimate=pl.CostEstimate(
            flops=2 * back.shape[1] * rows * model, bytes_accessed=8 * rows * model, transcendentals=0
        ),
        name="rest_grad",
    )(returned, back, hidden, out_grad, gain, inverse, along, grad)


def query_kernel(
    scale, query_ref, grad_ref, key_ref, value_ref, here_ref, all_ref, lse_ref, delta_ref, result_ref
):
    count = key_ref.shape[0] * key_ref.shape[1]
    key = key_ref[...].reshape(count, HEAD_DIM)
    value = value_ref[...].reshape(count, HEAD_DIM)
    allowed = here_ref[:, :1] == all_ref[...]
    scores = dot_nt(query_ref[...], key) * scale
    attend = jnp.where(allowed, jnp.exp(scores - lse_ref[:, :1]), 0.0)
    attend_grad = dot_nt(grad_ref[...], value)
    score_grad = (attend * (attend_grad - delta_ref[:, :1])).astype(jnp.bfloat16)
    result_ref[...] = (dot(score_grad, key) * scale).astype(jnp.bfloat16)


def query_grads(query, grad, gathered, here, every, lse, delta, heads):
    rows = query.shape[0]
    n_ctx = gathered.shape[0]
    count = n_ctx * rows
    own = pl.BlockSpec((rows, HEAD_DIM), lambda h: (0, h))
    return pl.pallas_call(
        functools.partial(query_kernel, HEAD_DIM ** (-0.5)),
        grid=(heads,),
        in_specs=[
            own,
            own,
            pl.BlockSpec((n_ctx, None, rows, HEAD_DIM), lambda h: (0, 0, 0, h)),
            pl.BlockSpec((n_ctx, None, rows, HEAD_DIM), lambda h: (0, 1, 0, h)),
            pl.BlockSpec((rows, LANES), lambda h: (0, 0)),
            pl.BlockSpec((1, count), lambda h: (0, 0)),
            own,
            own,
        ],
        out_specs=own,
        out_shape=jax.ShapeDtypeStruct((rows, heads * HEAD_DIM), jnp.bfloat16),
        compiler_params=params(40),
        cost_estimate=pl.CostEstimate(
            flops=6 * rows * count * heads * HEAD_DIM,
            bytes_accessed=4 * count * heads * HEAD_DIM,
            transcendentals=rows * count * heads,
        ),
        name="query_grads",
    )(query, grad, gathered, gathered, here, every, lse, delta)


def key_kernel(
    scale, chunk, key_ref, value_ref, query_ref, grad_ref, here_ref, all_ref, key_out_ref, value_out_ref
):
    n_ctx, rows = query_ref.shape[0], query_ref.shape[1]
    key, value = key_ref[...], value_ref[...]
    here = here_ref[:, :1]
    key_sum = value_sum = 0.0
    for start in range(0, n_ctx, chunk):
        blocks = slice(start, start + chunk)
        query = query_ref[blocks].reshape(chunk * rows, HEAD_DIM)
        grad = grad_ref[blocks, :rows, :].reshape(chunk * rows, HEAD_DIM)
        delta, lse = [], []
        for b in range(start, start + chunk):
            extra = grad_ref[b, rows:, :].astype(jnp.float32)
            delta.append(extra[0:1] + extra[1:2] + extra[2:3])
            lse.append(extra[3:4] + extra[4:5] + extra[5:6])
        delta = jnp.concatenate(delta, 1)
        lse = jnp.concatenate(lse, 1)
        allowed = here == all_ref[:, start * rows : (start + chunk) * rows]
        scores = dot_nt(key, query) * scale
        attend = jnp.where(allowed, jnp.exp(scores - lse), 0.0)
        score_grad = (attend * (dot_nt(value, grad) - delta)).astype(jnp.bfloat16)
        value_sum += dot(attend.astype(jnp.bfloat16), grad)
        key_sum += dot(score_grad, query)
    key_out_ref[...] = (key_sum * scale).astype(jnp.bfloat16)
    value_out_ref[...] = value_sum.astype(jnp.bfloat16)


def key_grads(key, value, gathered, grads, here, every, heads):
    rows = key.shape[0]
    n_ctx = gathered.shape[0]
    count = n_ctx * rows
    own = pl.BlockSpec((rows, HEAD_DIM), lambda h: (0, h))
    return pl.pallas_call(
        functools.partial(key_kernel, HEAD_DIM ** (-0.5), 4),
        grid=(heads,),
        in_specs=[
            own,
            own,
            pl.BlockSpec((n_ctx, None, rows, HEAD_DIM), lambda h: (0, 2, 0, h)),
            pl.BlockSpec((n_ctx, grads.shape[1], HEAD_DIM), lambda h: (0, 0, h)),
            pl.BlockSpec((rows, LANES), lambda h: (0, 0)),
            pl.BlockSpec((1, count), lambda h: (0, 0)),
        ],
        out_specs=[own, own],
        out_shape=[jax.ShapeDtypeStruct((rows, heads * HEAD_DIM), jnp.bfloat16)] * 2,
        compiler_params=params(40),
        cost_estimate=pl.CostEstimate(
            flops=8 * rows * count * heads * HEAD_DIM,
            bytes_accessed=4 * count * heads * HEAD_DIM,
            transcendentals=rows * count * heads,
        ),
        name="key_grads",
    )(key, value, gathered, grads, here, every)


def body(
    queries, keys, values, segments, hidden_state, norm_gain,
    route_gates, routes, out_grad, w_gate, w_up, w_down,
):
    rows, model = hidden_state.shape[1:]
    front = queries.shape[2]
    heads = front // HEAD_DIM
    n_exp = lax.axis_size("exp")
    capacity = 3 * rows * TOP // (2 * n_exp)
    hidden, grad_in = hidden_state[0], out_grad[0]
    gain = norm_gain[None, :]
    query, key, value = queries[0], keys[0], values[0]
    gate_mat, up_mat, down_mat = w_gate[0], w_up[0], w_down[0]
    here = lax.dynamic_slice_in_dim(segments[0], lax.axis_index("ctx") * rows, rows)
    here = jnp.broadcast_to(here[:, None], (rows, LANES))

    def exchange(x):
        cut = x.reshape(n_exp, capacity, x.shape[1])
        return lax.all_to_all(cut, "exp", split_axis=0, concat_axis=0, tiled=True).reshape(x.shape)

    gathered = lax.all_gather(jnp.stack([key, value, query]), "ctx")
    send, back, inverse = pack(routes[0].T, route_gates[0].T, hidden, gain, grad_in, n_exp, capacity)
    arrived = exchange(send)
    first, gate_grad, up_grad = expert(arrived, gate_mat, up_mat, down_mat, front)
    first = exchange(first)
    second = dot_nt(gate_grad, gate_mat[front:]) + dot_nt(up_grad, up_mat[front:])
    second = second.astype(jnp.bfloat16)
    out, lse, lse_rows = attend_own(query, gathered, here, segments, heads)
    grad, delta, along = front_grad(
        first, back, hidden, grad_in, gain, inverse, out, lse_rows, heads
    )
    grads = lax.all_gather(grad, "ctx")
    second = exchange(second)
    query_grad = query_grads(query, grad, gathered, here, segments, lse, delta, heads)
    residual_grad = rest_grad(second, back, hidden, grad_in, gain, inverse, along, grad)
    key_grad, value_grad = key_grads(key, value, gathered, grads, here, segments, heads)
    return (query_grad[None], key_grad[None], value_grad[None], residual_grad[None])


def solution(mesh):
    rows = P("exp", "ctx", None)
    mats = P("exp", None, None)
    in_specs = (rows, rows, rows, P("exp", None), rows, P(), rows, rows, rows, mats, mats, mats)
    return jax.shard_map(
        body, mesh=mesh, in_specs=in_specs, out_specs=(rows,) * 4, check_vma=False
    )
```

```python
import functools

import jax
import jax.numpy as jnp
from jax import lax
from jax.experimental import pallas as pl
from jax.experimental.pallas import tpu as pltpu
from jax.sharding import PartitionSpec as P

HEAD_DIM = 128
TOP = 2
EPSILON = 1e-06
MASKED = -1e30
LANES = 128
NT = (((1,), (1,)), ((), ()))
MIB = 1 << 20
VMEM = pltpu.MemorySpace.VMEM


def params(limit_mib, **more):
    return pltpu.CompilerParams(vmem_limit_bytes=limit_mib * MIB, **more)


def dot(a, b):
    return jnp.dot(a, b, preferred_element_type=jnp.float32)


def dot_nt(a, b):
    return lax.dot_general(a, b, NT, preferred_element_type=jnp.float32)


def three_parts(x):
    high = x.astype(jnp.bfloat16)
    rest = x - high.astype(jnp.float32)
    mid = rest.astype(jnp.bfloat16)
    low = (rest - mid.astype(jnp.float32)).astype(jnp.bfloat16)
    return high, mid, low


def column_of(row):
    size = row.shape[1]
    return jnp.broadcast_to(row.astype(jnp.float32), (size, size)).T


def pack_kernel(
    n_exp, capacity, block,
    routes_ref, gates_ref, hidden_ref, gain_ref, out_grad_ref,
    send_ref, back_ref, inverse_ref,
    rows_scr, pick_scr,
):
    step = pl.program_id(0)
    rows, model = hidden_ref.shape
    slots = n_exp * capacity

    @pl.when(step == 0)
    def _():
        hidden = hidden_ref[...].astype(jnp.float32)
        inverse = lax.rsqrt(jnp.mean(hidden * hidden, -1, keepdims=True) + EPSILON)
        inverse_ref[...] = jnp.broadcast_to(inverse, inverse_ref.shape)
        normed = (hidden * inverse * gain_ref[...]).astype(jnp.bfloat16)
        out_grad = out_grad_ref[...].astype(jnp.float32)
        expert_id = lax.broadcasted_iota(jnp.int32, (n_exp, rows), 0)
        earlier = (
            lax.broadcasted_iota(jnp.int32, (rows, rows), 0)
            < lax.broadcasted_iota(jnp.int32, (rows, rows), 1)
        ).astype(jnp.bfloat16)
        slot_id = lax.broadcasted_iota(jnp.int32, (slots, rows), 0).astype(jnp.float32)
        first_slot = expert_id.astype(jnp.float32) * capacity
        total = None
        for j in range(TOP):
            part = slice(j * rows, (j + 1) * rows)
            named = (expert_id == routes_ref[j : j + 1, :]).astype(jnp.float32)
            place = first_slot + dot(named.astype(jnp.bfloat16), earlier)
            if j:
                place = place + used
            target = jnp.sum(named * place, 0, keepdims=True)
            pick = (slot_id == target).astype(jnp.float32)
            pick_scr[:, part] = pick.astype(jnp.bfloat16)
            total = pick if total is None else total + pick
            if j == 0:
                used = jnp.sum(named, 1, keepdims=True)
            gate = jnp.broadcast_to(gates_ref[j : j + 1, :], (rows, rows)).T[:, :1]
            rows_scr[part, :model] = normed
            rows_scr[part, model:] = (gate * out_grad).astype(jnp.bfloat16)
        back_ref[...] = total.T.astype(jnp.bfloat16)

    pick = pick_scr[pl.ds(pl.multiple_of(step * block, block), block), :]
    send_ref[...] = dot(pick, rows_scr[...]).astype(jnp.bfloat16)


def pack(routes_t, gates_t, hidden, gain, out_grad, n_exp, capacity):
    rows, model = hidden.shape
    slots = n_exp * capacity
    block = slots // 2
    whole = lambda shape: pl.BlockSpec(shape, lambda i: (0,) * len(shape))
    return pl.pallas_call(
        functools.partial(pack_kernel, n_exp, capacity, block),
        grid=(slots // block,),
        in_specs=[
            whole((TOP, rows)),
            whole((TOP, rows)),
            whole((rows, model)),
            whole((1, model)),
            whole((rows, model)),
        ],
        out_specs=[
            pl.BlockSpec((block, 2 * model), lambda i: (i, 0)),
            whole((rows, slots)),
            whole((rows, LANES)),
        ],
        out_shape=[
            jax.ShapeDtypeStruct((slots, 2 * model), jnp.bfloat16),
            jax.ShapeDtypeStruct((rows, slots), jnp.bfloat16),
            jax.ShapeDtypeStruct((rows, LANES), jnp.float32),
        ],
        scratch_shapes=[
            pltpu.VMEM((TOP * rows, 2 * model), jnp.bfloat16),
            pltpu.VMEM((slots, TOP * rows), jnp.bfloat16),
        ],
        compiler_params=params(60),
        cost_estimate=pl.CostEstimate(
            flops=8 * slots * rows * model, bytes_accessed=8 * slots * model, transcendentals=0
        ),
        name="pack_rows",
    )(routes_t, gates_t, hidden, gain, out_grad)


def expert_kernel(
    model, front,
    rows_in, gate_in, up_in, down_in,
    front_ref, gate_grad_ref, up_grad_ref,
    rows_ref, gate_ref, up_ref, down_ref, sems,
):
    copies = [
        pltpu.make_async_copy(source, target, sems.at[i])
        for i, (source, target) in enumerate(
            ((rows_in, rows_ref), (gate_in, gate_ref), (up_in, up_ref), (down_in, down_ref))
        )
    ]
    for copy in copies:
        copy.start()
    copies[0].wait()
    copies[1].wait()
    gate_pre = dot(rows_ref[:, :model], gate_ref[...])
    copies[2].wait()
    up_pre = dot(rows_ref[:, :model], up_ref[...])
    copies[3].wait()
    hidden_grad = dot_nt(rows_ref[:, model:], down_ref[...])
    sigmoid = jax.nn.sigmoid(gate_pre)
    slope = sigmoid * (1.0 + gate_pre * (1.0 - sigmoid))
    gate_grad = (hidden_grad * up_pre * slope).astype(jnp.bfloat16)
    up_grad = (hidden_grad * gate_pre * sigmoid).astype(jnp.bfloat16)
    gate_grad_ref[...] = gate_grad
    up_grad_ref[...] = up_grad
    along = jnp.sum(
        gate_grad.astype(jnp.float32) * gate_pre + up_grad.astype(jnp.float32) * up_pre,
        -1,
        keepdims=True,
    )
    part = dot_nt(gate_grad, gate_ref[:front, :]) + dot_nt(up_grad, up_ref[:front, :])
    front_ref[:, :front] = part.astype(jnp.bfloat16)
    whole = jnp.broadcast_to(along, (along.shape[0], LANES))
    high = whole.astype(jnp.bfloat16).astype(jnp.float32)
    lane = lax.broadcasted_iota(jnp.int32, whole.shape, 1)
    tail = jnp.where(lane == 0, high, jnp.where(lane == 1, whole - high, 0.0))
    front_ref[:, front:] = tail.astype(jnp.bfloat16)


def expert(rows, gate_mat, up_mat, down_mat, front):
    slots = rows.shape[0]
    model, units = gate_mat.shape
    operands = (rows, gate_mat, up_mat, down_mat)
    return pl.pallas_call(
        functools.partial(expert_kernel, model, front),
        in_specs=[pl.BlockSpec(memory_space=pl.ANY)] * 4,
        out_shape=[
            jax.ShapeDtypeStruct((slots, front + LANES), jnp.bfloat16),
            jax.ShapeDtypeStruct((slots, units), jnp.bfloat16),
            jax.ShapeDtypeStruct((slots, units), jnp.bfloat16),
        ],
        scratch_shapes=[pltpu.VMEM(x.shape, x.dtype) for x in operands]
        + [pltpu.SemaphoreType.DMA((4,))],
        compiler_params=params(60),
        cost_estimate=pl.CostEstimate(
            flops=2 * slots * units * (3 * model + 2 * front),
            bytes_accessed=6 * model * units + 4 * slots * model,
            transcendentals=slots * units,
        ),
        name="expert_rows",
    )(*operands)


def second_kernel(gate_grad_ref, up_grad_ref, gate_ref, up_ref, second_ref):
    second_ref[...] = (
        dot_nt(gate_grad_ref[...], gate_ref[...]) + dot_nt(up_grad_ref[...], up_ref[...])
    ).astype(jnp.bfloat16)


def second_rows(gate_grad, up_grad, gate_mat, up_mat, front):
    slots, units = gate_grad.shape
    width = 512
    rest = gate_mat.shape[0] - front
    whole = pl.BlockSpec((slots, units), lambda i: (0, 0))
    mat = pl.BlockSpec((width, units), lambda i: (front // width + i, 0))
    return pl.pallas_call(
        second_kernel,
        grid=(rest // width,),
        in_specs=[whole, whole, mat, mat],
        out_specs=pl.BlockSpec((slots, width), lambda i: (0, i)),
        out_shape=jax.ShapeDtypeStruct((slots, rest), jnp.bfloat16),
        compiler_params=params(60),
        cost_estimate=pl.CostEstimate(
            flops=4 * slots * units * rest, bytes_accessed=4 * rest * units, transcendentals=0
        ),
        name="second_rows",
    )(gate_grad, up_grad, gate_mat, up_mat)


NEAR = ((0, 0), (0, 1), (3, 0), (1, 0))
FAR = ((2, 0), (1, 1), (3, 1), (2, 1))


def source_of(ctx, place):
    chip = lax.div(ctx, 2)
    x = lax.rem(lax.div(chip, 2) + place[0], 4)
    y = lax.rem(lax.rem(chip, 2) + place[1], 2)
    return 2 * x + y


def ids_in_order(ctx, every_ref):
    core = lax.rem(ctx, 2)
    parts = [every_ref[2 * source_of(ctx, place) + core] for place in NEAR + FAR]
    parts += [every_ref[2 * source_of(ctx, place) + 1 - core] for place in NEAR + FAR]
    return jnp.concatenate(parts, 1).astype(jnp.float32)


def attend_kernel(scale, heads, pieces, ctx_ref, query_ref, every_ref, *refs):
    number = sum(pieces)
    own_refs, other_refs, refs = refs[:number], refs[number : 2 * number], refs[2 * number :]
    out_ref, attend_ref, row_ref, key_ref, value_ref, far_key_ref, far_value_ref = refs[:7]
    here_scr, every_scr = refs[7:]
    rows = query_ref.shape[0]

    @pl.when(pl.program_id(0) == 0)
    def _():
        here_scr[...] = column_of(every_ref[ctx_ref[0]])
        every_scr[...] = ids_in_order(ctx_ref[0], every_ref)

    allowed = here_scr[:, :1] == every_scr[...]
    for h in range(heads):
        columns = slice(h * HEAD_DIM, (h + 1) * HEAD_DIM)
        for blocks, outs in (
            (own_refs, (key_ref, value_ref)), (other_refs, (far_key_ref, far_value_ref))
        ):
            for place, count in enumerate(pieces):
                start = sum(pieces[:place])
                for which, out in enumerate(outs):
                    if count == 1:
                        part = blocks[start][which * rows : (which + 1) * rows, columns]
                    else:
                        part = blocks[start + which][:, columns]
                    out[h, place * rows : (place + 1) * rows, :] = part
        key = jnp.concatenate([key_ref[h], far_key_ref[h]], 0)
        value = jnp.concatenate([value_ref[h], far_value_ref[h]], 0)
        scores = jnp.where(allowed, dot_nt(query_ref[:, columns], key) * scale, MASKED)
        peak = jnp.max(scores, -1, keepdims=True)
        attend = jnp.where(allowed, jnp.exp(scores - peak), 0.0)
        summed = jnp.sum(attend, -1, keepdims=True)
        attend = (attend * (1.0 / summed)).astype(jnp.bfloat16)
        attend_ref[h] = attend
        out_ref[:, columns] = dot(attend, value)
        lse = jnp.broadcast_to(peak + jnp.log(summed), here_scr.shape)
        row_ref[h] = lse.T[:8, :]


def attend_own(ctx, query, every, pieces, own_blocks, other_blocks, heads):
    rows, front = query.shape
    n_ctx = every.shape[0]
    count = n_ctx * rows
    each = 2
    own = pl.BlockSpec((rows, each * HEAD_DIM), lambda h, ctx: (0, h))
    half = pl.BlockSpec((each, count // 2, HEAD_DIM), lambda h, ctx: (h, 0, 0))
    blocks = (*own_blocks, *other_blocks)
    return pl.pallas_call(
        functools.partial(attend_kernel, HEAD_DIM ** (-0.5), each, pieces),
        grid_spec=pltpu.PrefetchScalarGridSpec(
            num_scalar_prefetch=1,
            grid=(heads // each,),
            in_specs=[own, pl.BlockSpec((n_ctx, 1, rows), lambda h, ctx: (0, 0, 0))]
            + [
                pl.BlockSpec((block.shape[0], each * HEAD_DIM), lambda h, ctx: (0, h))
                for block in blocks
            ],
            out_specs=[
                own,
                pl.BlockSpec((each, rows, count), lambda h, ctx: (h, 0, 0)),
                pl.BlockSpec((each, 8, rows), lambda h, ctx: (h, 0, 0)),
            ]
            + [half] * 4,
            scratch_shapes=[
                pltpu.VMEM((rows, LANES), jnp.float32),
                pltpu.VMEM((1, count), jnp.float32),
            ],
        ),
        out_shape=[
            jax.ShapeDtypeStruct((rows, front), jnp.float32),
            jax.ShapeDtypeStruct((heads, rows, count), jnp.bfloat16),
            jax.ShapeDtypeStruct((heads, 8, rows), jnp.float32),
        ]
        + [jax.ShapeDtypeStruct((heads, count // 2, HEAD_DIM), jnp.bfloat16)] * 4,
        compiler_params=params(60),
        cost_estimate=pl.CostEstimate(
            flops=4 * rows * count * front,
            bytes_accessed=8 * count * front,
            transcendentals=rows * count * heads,
        ),
        name="attend_own",
    )(ctx, query, every, *blocks)


def front_kernel(
    model, heads,
    returned_ref, back_ref, hidden_ref, out_grad_ref, gain_ref, inverse_ref, out_ref, lse_ref,
    grad_ref, delta_ref, along_ref, residual_ref,
):
    front = heads * HEAD_DIM
    rows = hidden_ref.shape[0]
    inverse = inverse_ref[:, :1]
    sums = dot(back_ref[...], returned_ref[...])
    along = jnp.sum(sums[:, front:], -1, keepdims=True) * (1.0 / model)
    along_ref[...] = jnp.broadcast_to(along, along_ref.shape)
    weighted = gain_ref[...] * sums[:, :front]
    hidden = hidden_ref[...].astype(jnp.float32)
    residual = out_grad_ref[...].astype(jnp.float32) + inverse * weighted
    residual = residual - hidden * (inverse * inverse * along)
    grad = residual.astype(jnp.bfloat16)
    grad_ref[:rows, :] = grad
    residual_ref[...] = grad
    product = grad.astype(jnp.float32) * out_ref[...]
    pad = jnp.zeros((grad_ref.shape[0] - rows - 6, rows), jnp.bfloat16)
    for h in range(heads):
        columns = slice(h * HEAD_DIM, (h + 1) * HEAD_DIM)
        delta = jnp.broadcast_to(jnp.sum(product[:, columns], -1, keepdims=True), (rows, rows))
        delta_ref[:, columns] = delta
        parts = three_parts(delta.T[:1, :]) + three_parts(lse_ref[h][:1, :])
        parts = [part.astype(jnp.float32) for part in parts] + [pad.astype(jnp.float32)]
        grad_ref[rows:, columns] = jnp.concatenate(parts, 0).astype(jnp.bfloat16)


def front_grad(returned, back, hidden, out_grad, gain, inverse, out, lse_rows, heads):
    rows, model = hidden.shape
    slots = back.shape[1]
    front = heads * HEAD_DIM
    extra = 16
    whole = lambda shape: pl.BlockSpec(shape, lambda i: (0,) * len(shape))
    return pl.pallas_call(
        functools.partial(front_kernel, model, heads),
        grid=(1,),
        in_specs=[
            whole((slots, front + LANES)),
            whole((rows, slots)),
            whole((rows, front)),
            whole((rows, front)),
            whole((1, front)),
            whole((rows, LANES)),
            whole((rows, front)),
            whole((heads, 8, rows)),
        ],
        out_specs=[
            whole((rows + extra, front)),
            whole((rows, front)),
            whole((rows, LANES)),
            whole((rows, front)),
        ],
        out_shape=[
            jax.ShapeDtypeStruct((rows + extra, front), jnp.bfloat16),
            jax.ShapeDtypeStruct((rows, front), jnp.float32),
            jax.ShapeDtypeStruct((rows, LANES), jnp.float32),
            jax.ShapeDtypeStruct((rows, model), jnp.bfloat16),
        ],
        compiler_params=params(60),
        cost_estimate=pl.CostEstimate(
            flops=2 * slots * rows * front, bytes_accessed=6 * slots * front, transcendentals=0
        ),
        name="front_grad",
    )(returned, back, hidden, out_grad, gain, inverse, out, lse_rows)


def rest_kernel(
    returned_ref, back_ref, hidden_ref, out_grad_ref, gain_ref, inverse_ref, along_ref, _,
    residual_ref,
):
    inverse = inverse_ref[:, :1]
    weighted = gain_ref[...] * dot(back_ref[...], returned_ref[...])
    hidden = hidden_ref[...].astype(jnp.float32)
    residual = out_grad_ref[...].astype(jnp.float32) + inverse * weighted
    residual = residual - hidden * (inverse * inverse * along_ref[:, :1])
    residual_ref[...] = residual.astype(jnp.bfloat16)


def rest_grad(returned, back, hidden, out_grad, gain, inverse, along, residual):
    rows, model = hidden.shape
    slots, rest = returned.shape
    whole = lambda shape: pl.BlockSpec(shape, lambda i: (0,) * len(shape))
    second = pl.BlockSpec((rows, rest), lambda i: (0, 1))
    return pl.pallas_call(
        rest_kernel,
        grid=(1,),
        in_specs=[
            whole((slots, rest)),
            whole((rows, slots)),
            second,
            second,
            pl.BlockSpec((1, rest), lambda i: (0, 1)),
            whole((rows, LANES)),
            whole((rows, LANES)),
            pl.BlockSpec(memory_space=pl.ANY),
        ],
        out_specs=second,
        out_shape=jax.ShapeDtypeStruct((rows, model), jnp.bfloat16),
        input_output_aliases={7: 0},
        compiler_params=params(60),
        cost_estimate=pl.CostEstimate(
            flops=2 * slots * rows * rest, bytes_accessed=8 * rows * model, transcendentals=0
        ),
        name="rest_grad",
    )(returned, back, hidden, out_grad, gain, inverse, along, residual)


def query_kernel(
    scale, heads,
    grad_ref, attend_ref, key_ref, value_ref, far_key_ref, far_value_ref, delta_ref, *refs
):
    result_ref = refs[-1]
    for h in range(heads):
        columns = slice(h * HEAD_DIM, (h + 1) * HEAD_DIM)
        key = jnp.concatenate([key_ref[h], far_key_ref[h]], 0)
        value = jnp.concatenate([value_ref[h], far_value_ref[h]], 0)
        attend_grad = dot_nt(grad_ref[:, columns], value)
        delta = delta_ref[:, columns][:, :1]
        score_grad = attend_ref[h].astype(jnp.float32) * (attend_grad - delta)
        result_ref[:, columns] = (dot(score_grad.astype(jnp.bfloat16), key) * scale).astype(
            jnp.bfloat16
        )


def query_grads(grad, attend, key, value, far_key, far_value, delta, first, heads, before):
    total, rows, count = attend.shape
    each = 2
    skip = first // each
    own = pl.BlockSpec((rows, each * HEAD_DIM), lambda h: (0, skip + h))
    half = pl.BlockSpec((each, count // 2, HEAD_DIM), lambda h: (skip + h, 0, 0))
    return pl.pallas_call(
        functools.partial(query_kernel, HEAD_DIM ** (-0.5), each),
        grid=(heads // each,),
        in_specs=[own, pl.BlockSpec((each, rows, count), lambda h: (skip + h, 0, 0))]
        + [half] * 4
        + [own]
        + [pl.BlockSpec(memory_space=pl.ANY)] * len(before),
        out_specs=own,
        out_shape=jax.ShapeDtypeStruct((rows, total * HEAD_DIM), jnp.bfloat16),
        input_output_aliases={7: 0} if before else {},
        compiler_params=params(60),
        cost_estimate=pl.CostEstimate(
            flops=4 * rows * count * heads * HEAD_DIM,
            bytes_accessed=6 * count * heads * HEAD_DIM,
            transcendentals=0,
        ),
        name="query_grads",
    )(grad, attend, key, value, far_key, far_value, delta, *before)


def key_kernel(
    scale, heads, places, pieces, query_pieces, last,
    ctx_ref, key_ref, value_ref, far_key_ref, far_value_ref, every_ref, *refs
):
    query_refs, refs = refs[: sum(query_pieces)], refs[sum(query_pieces) :]
    grad_refs, refs = refs[: sum(pieces)], refs[sum(pieces) :]
    rows = key_ref.shape[1]
    ctx = ctx_ref[0]
    core = lax.rem(ctx, 2)
    chip = lax.div(ctx, 2)
    here_scr, refs = refs[-1], refs[:-1]

    @pl.when(pl.program_id(0) == 0)
    def _():
        here_scr[:rows, :] = column_of(every_ref[ctx])
        here_scr[rows:, :] = column_of(every_ref[2 * chip + 1 - core])

    here = here_scr[:, :1]
    parts, every = [], []
    for i, place in enumerate(places):
        start = sum(pieces[:i])
        parts.append(
            jnp.concatenate([ref[...] for ref in grad_refs[start : start + pieces[i]]], 0)
        )
        every.append(every_ref[2 * source_of(ctx, place) + core])
    extra = jnp.concatenate([part[rows:] for part in parts], 1).astype(jnp.float32)
    delta = extra[0:1] + extra[1:2] + extra[2:3]
    lse = extra[3:4] + extra[4:5] + extra[5:6]
    allowed = here == jnp.concatenate(every, 1).astype(jnp.float32)
    width = parts[0].shape[1]
    for h in range(heads):
        columns = slice(h * HEAD_DIM, (h + 1) * HEAD_DIM)

        def lanes(row):
            starts = [i * width + h * HEAD_DIM for i in range(len(places))]
            return jnp.concatenate([row[:, i : i + HEAD_DIM] for i in starts], 1)

        key = jnp.concatenate([key_ref[h], far_key_ref[h]], 0)
        value = jnp.concatenate([value_ref[h], far_value_ref[h]], 0)
        query = jnp.concatenate([ref[:, columns] for ref in query_refs], 0)
        grad = jnp.concatenate([part[:rows, columns] for part in parts], 0)
        scores = dot_nt(key, query) * scale
        attend = jnp.where(allowed, jnp.exp(scores - lanes(lse)), 0.0)
        score_grad = attend * (dot_nt(value, grad) - lanes(delta))
        value_part = dot(attend.astype(jnp.bfloat16), grad)
        key_part = dot(score_grad.astype(jnp.bfloat16), query)
        if last:
            key_in, value_in, own_ref, other_ref = refs
            key_part = (key_in[h] + key_part) * scale
            value_part = value_in[h] + value_part
            own_ref[0, h] = key_part[:rows]
            own_ref[1, h] = value_part[:rows]
            other_ref[0, h] = key_part[rows:].astype(jnp.bfloat16)
            other_ref[1, h] = value_part[rows:].astype(jnp.bfloat16)
        else:
            key_out, value_out = refs
            key_out[h] = key_part
            value_out[h] = value_part


def key_grads(
    ctx, key, value, far_key, far_value, every, query_pieces, queries, pieces, grads, sums
):
    heads = key.shape[0]
    n_ctx, _, rows = every.shape
    last = sums is not None
    each = 2
    width = each * HEAD_DIM
    places = FAR if last else NEAR
    counted = len(places) * rows
    mine = pl.BlockSpec((each, rows, HEAD_DIM), lambda h, ctx: (h, 0, 0))
    piece_specs = [
        pl.BlockSpec((piece.shape[0], width), lambda h, ctx: (0, h)) for piece in (*queries, *grads)
    ]
    sum_spec = pl.BlockSpec((each, 2 * rows, HEAD_DIM), lambda h, ctx: (h, 0, 0))
    pair_spec = pl.BlockSpec((2, each, rows, HEAD_DIM), lambda h, ctx: (0, h, 0, 0))
    sum_shape = (heads, 2 * rows, HEAD_DIM)
    pair_shape = (2, heads, rows, HEAD_DIM)
    here = [pltpu.VMEM((2 * rows, LANES), jnp.float32)]
    if last:
        extra_in = [sum_spec, sum_spec]
        out_specs = [pair_spec, pair_spec]
        out_shape = [
            jax.ShapeDtypeStruct(pair_shape, jnp.float32),
            jax.ShapeDtypeStruct(pair_shape, jnp.bfloat16),
        ]
    else:
        extra_in = []
        out_specs = [sum_spec, sum_spec]
        out_shape = [jax.ShapeDtypeStruct(sum_shape, jnp.float32)] * 2
    return pl.pallas_call(
        functools.partial(
            key_kernel, HEAD_DIM ** (-0.5), each, places, pieces, query_pieces, last
        ),
        grid_spec=pltpu.PrefetchScalarGridSpec(
            num_scalar_prefetch=1,
            grid=(heads // each,),
            in_specs=[mine] * 4
            + [
                pl.BlockSpec((n_ctx, 1, rows), lambda h, ctx: (0, 0, 0)),
            ]
            + piece_specs
            + extra_in,
            out_specs=out_specs,
            scratch_shapes=here,
        ),
        out_shape=out_shape,
        compiler_params=params(60),
        cost_estimate=pl.CostEstimate(
            flops=16 * rows * counted * heads * HEAD_DIM,
            bytes_accessed=8 * counted * heads * HEAD_DIM,
            transcendentals=2 * rows * counted * heads,
        ),
        name="key_grads_last" if last else "key_grads_first",
    )(ctx, key, value, far_key, far_value, every, *queries, *grads, *(sums or ()))


def finish_kernel(own_ref, arrived_ref, key_ref, value_ref):
    total = own_ref[...] + arrived_ref[...].astype(jnp.float32)
    for h in range(own_ref.shape[1]):
        columns = slice(h * HEAD_DIM, (h + 1) * HEAD_DIM)
        key_ref[:, columns] = total[0, h].astype(jnp.bfloat16)
        value_ref[:, columns] = total[1, h].astype(jnp.bfloat16)


def finish(own, arrived):
    _, heads, rows, size = own.shape
    each = 4
    pair = pl.BlockSpec((2, each, rows, size), lambda h: (0, h, 0, 0))
    return pl.pallas_call(
        finish_kernel,
        grid=(heads // each,),
        in_specs=[pair, pair],
        out_specs=[pl.BlockSpec((rows, each * size), lambda h: (0, h))] * 2,
        out_shape=[jax.ShapeDtypeStruct((rows, heads * size), jnp.bfloat16)] * 2,
        compiler_params=params(60),
        name="finish",
    )(own, arrived)


def body(
    queries, keys, values, segments, hidden_state, norm_gain,
    route_gates, routes, out_grad, w_gate, w_up, w_down,
):
    rows, model = hidden_state.shape[1:]
    front = queries.shape[2]
    heads = front // HEAD_DIM
    n_exp = lax.axis_size("exp")
    capacity = 3 * rows * TOP // (2 * n_exp)
    hidden, grad_in = hidden_state[0], out_grad[0]
    gain = norm_gain[None, :]
    query, key, value = queries[0], keys[0], values[0]
    gate_mat, up_mat, down_mat = w_gate[0], w_up[0], w_down[0]
    n_ctx = lax.axis_size("ctx")
    ctx = lax.axis_index("ctx")[None]
    every = segments[0].reshape(n_ctx, 1, rows)

    def exchange(x):
        cut = x.reshape(n_exp, capacity, x.shape[1])
        return lax.all_to_all(cut, "exp", split_axis=0, concat_axis=0, tiled=True).reshape(x.shape)

    def right(x):
        return lax.ppermute(x, "ctx", [(i, (i + 4) % n_ctx) for i in range(n_ctx)])

    def left(x):
        return lax.ppermute(x, "ctx", [(i, (i - 4) % n_ctx) for i in range(n_ctx)])

    def across(x):
        return lax.ppermute(x, "ctx", [(i, i ^ 2) for i in range(n_ctx)])

    def swap_core(x):
        return lax.ppermute(x, "ctx", [(i, i ^ 1) for i in range(n_ctx)])

    def first_round(x):
        return across(x), right(x), left(x)

    def second_round(from_y, from_left, from_right):
        return right(from_left), left(from_y), across(from_left)

    def third_round(far, y_right, y_left):
        cut = far.shape[0] // 3
        return across(far[:cut]), left(y_right[cut : 2 * cut]), right(y_left[2 * cut :])

    send, back, inverse = pack(
        routes[0].T, route_gates[0].T, hidden, gain, grad_in, n_exp, capacity
    )
    def spread(x, near):
        half = x.shape[0] // 2
        from_y, from_left, from_right = near
        far = (right(from_left[:half]), left(from_right[half:]))
        y_right, y_left = left(from_y), right(from_y)
        last = (right(y_left[:half]), left(y_right[half:]))
        return (x, *near, *far, y_right, y_left, *last)

    pieces = (1, 1, 1, 1, 2, 1, 1, 2)
    key, value, query, inverse = lax.optimization_barrier((key, value, query, inverse))
    arrived = exchange(send)
    stacked = jnp.concatenate([key, value], 0)
    blocks = spread(stacked, first_round(stacked))
    other_blocks = [swap_core(block) for block in blocks]
    query_near = first_round(query)
    number = len(blocks)
    arrived, *all_blocks = lax.optimization_barrier(
        (arrived, *blocks, *other_blocks, *query_near)
    )
    blocks, other_blocks = all_blocks[:number], all_blocks[number : 2 * number]
    query_near = all_blocks[2 * number :]
    first, gate_grad, up_grad = expert(arrived, gate_mat, up_mat, down_mat, front)
    first = exchange(first)
    query, gate_grad = lax.optimization_barrier((query, gate_grad))
    query_parts = spread(query, query_near)
    second = second_rows(gate_grad, up_grad, gate_mat, up_mat, front)
    out, attend, lse_rows, *held = attend_own(
        ctx, query, every, pieces, blocks, other_blocks, heads
    )
    first, second, *query_parts = lax.optimization_barrier((first, second, *query_parts))
    grad, delta, along, residual = front_grad(
        first, back, hidden, grad_in, gain, inverse, out, lse_rows, heads
    )
    near = first_round(grad)
    half = heads // 2
    query_front = query_grads(grad, attend, *held, delta, 0, half, ())
    grad_then, query_front, *near = lax.optimization_barrier((grad, query_front, *near))
    far = second_round(*near)
    query_grad = query_grads(
        grad_then, attend, *held, delta, half, half, (query_front,)
    )
    held_back = lax.optimization_barrier((second, query_grad, *far, grad_then, *near))
    second, query_grad, far, near = held_back[0], held_back[1], held_back[2:5], held_back[5:]
    second = exchange(second)
    last = third_round(*far)
    sums = key_grads(
        ctx, *held, every, (1,) * 4, query_parts[:4], (1,) * 4, tuple(near), None
    )
    own, other = key_grads(
        ctx, *held, every, (2, 1, 1, 2), query_parts[4:], (1, 1, 1, 3), (*far, *last), sums
    )
    other = swap_core(other)
    residual_grad = rest_grad(second, back, hidden, grad_in, gain, inverse, along, residual)
    other, residual_grad = lax.optimization_barrier((other, residual_grad))
    key_grad, value_grad = finish(own, other)
    return (query_grad[None], key_grad[None], value_grad[None], residual_grad[None])


def solution(mesh):
    rows = P("exp", "ctx", None)
    mats = P("exp", None, None)
    in_specs = (rows, rows, rows, P("exp", None), rows, P(), rows, rows, rows, mats, mats, mats)
    return jax.shard_map(
        body, mesh=mesh, in_specs=in_specs, out_specs=(rows,) * 4, check_vma=False
    )
```

```python
import functools

import jax
import jax.numpy as jnp
from jax import lax
from jax.experimental import pallas as pl
from jax.experimental.pallas import tpu as pltpu
from jax.sharding import PartitionSpec as P

HEAD_DIM = 128
TOP = 2
EPSILON = 1e-06
MASKED = -1e30
LANES = 128
NT = (((1,), (1,)), ((), ()))
MIB = 1 << 20
VMEM = pltpu.MemorySpace.VMEM


def params(limit_mib, **more):
    return pltpu.CompilerParams(vmem_limit_bytes=limit_mib * MIB, **more)


def dot(a, b):
    return jnp.dot(a, b, preferred_element_type=jnp.float32)


def dot_nt(a, b):
    return lax.dot_general(a, b, NT, preferred_element_type=jnp.float32)


def three_parts(x):
    high = x.astype(jnp.bfloat16)
    rest = x - high.astype(jnp.float32)
    mid = rest.astype(jnp.bfloat16)
    low = (rest - mid.astype(jnp.float32)).astype(jnp.bfloat16)
    return high, mid, low


def column_of(row):
    size = row.shape[1]
    return jnp.broadcast_to(row.astype(jnp.float32), (size, size)).T


def pack_kernel(
    n_exp, capacity, block,
    routes_ref, gates_ref, hidden_ref, gain_ref, out_grad_ref,
    send_ref, back_ref, inverse_ref,
    rows_scr, pick_scr,
):
    step = pl.program_id(0)
    rows, model = hidden_ref.shape
    slots = n_exp * capacity

    @pl.when(step == 0)
    def _():
        hidden = hidden_ref[...].astype(jnp.float32)
        inverse = lax.rsqrt(jnp.mean(hidden * hidden, -1, keepdims=True) + EPSILON)
        inverse_ref[...] = jnp.broadcast_to(inverse, inverse_ref.shape)
        normed = (hidden * inverse * gain_ref[...]).astype(jnp.bfloat16)
        out_grad = out_grad_ref[...].astype(jnp.float32)
        expert_id = lax.broadcasted_iota(jnp.int32, (n_exp, rows), 0)
        earlier = (
            lax.broadcasted_iota(jnp.int32, (rows, rows), 0)
            < lax.broadcasted_iota(jnp.int32, (rows, rows), 1)
        ).astype(jnp.bfloat16)
        slot_id = lax.broadcasted_iota(jnp.int32, (slots, rows), 0).astype(jnp.float32)
        first_slot = expert_id.astype(jnp.float32) * capacity
        total = None
        for j in range(TOP):
            part = slice(j * rows, (j + 1) * rows)
            named = (expert_id == routes_ref[j : j + 1, :]).astype(jnp.float32)
            place = first_slot + dot(named.astype(jnp.bfloat16), earlier)
            if j:
                place = place + used
            target = jnp.sum(named * place, 0, keepdims=True)
            pick = (slot_id == target).astype(jnp.float32)
            pick_scr[:, part] = pick.astype(jnp.bfloat16)
            total = pick if total is None else total + pick
            if j == 0:
                used = jnp.sum(named, 1, keepdims=True)
            gate = jnp.broadcast_to(gates_ref[j : j + 1, :], (rows, rows)).T[:, :1]
            rows_scr[part, :model] = normed
            rows_scr[part, model:] = (gate * out_grad).astype(jnp.bfloat16)
        back_ref[...] = total.T.astype(jnp.bfloat16)

    pick = pick_scr[pl.ds(pl.multiple_of(step * block, block), block), :]
    send_ref[...] = dot(pick, rows_scr[...]).astype(jnp.bfloat16)


def pack(routes_t, gates_t, hidden, gain, out_grad, n_exp, capacity):
    rows, model = hidden.shape
    slots = n_exp * capacity
    block = slots // 2
    whole = lambda shape: pl.BlockSpec(shape, lambda i: (0,) * len(shape))
    return pl.pallas_call(
        functools.partial(pack_kernel, n_exp, capacity, block),
        grid=(slots // block,),
        in_specs=[
            whole((TOP, rows)),
            whole((TOP, rows)),
            whole((rows, model)),
            whole((1, model)),
            whole((rows, model)),
        ],
        out_specs=[
            pl.BlockSpec((block, 2 * model), lambda i: (i, 0)),
            whole((rows, slots)),
            whole((rows, LANES)),
        ],
        out_shape=[
            jax.ShapeDtypeStruct((slots, 2 * model), jnp.bfloat16),
            jax.ShapeDtypeStruct((rows, slots), jnp.bfloat16),
            jax.ShapeDtypeStruct((rows, LANES), jnp.float32),
        ],
        scratch_shapes=[
            pltpu.VMEM((TOP * rows, 2 * model), jnp.bfloat16),
            pltpu.VMEM((slots, TOP * rows), jnp.bfloat16),
        ],
        compiler_params=params(60),
        cost_estimate=pl.CostEstimate(
            flops=8 * slots * rows * model, bytes_accessed=8 * slots * model, transcendentals=0
        ),
        name="pack_rows",
    )(routes_t, gates_t, hidden, gain, out_grad)


def expert_kernel(
    model, front,
    rows_in, gate_in, up_in, down_in,
    front_ref, gate_grad_ref, up_grad_ref,
    rows_ref, gate_ref, up_ref, down_ref, sems,
):
    copies = [
        pltpu.make_async_copy(source, target, sems.at[i])
        for i, (source, target) in enumerate(
            ((rows_in, rows_ref), (gate_in, gate_ref), (up_in, up_ref), (down_in, down_ref))
        )
    ]
    for copy in copies:
        copy.start()
    copies[0].wait()
    copies[1].wait()
    gate_pre = dot(rows_ref[:, :model], gate_ref[...])
    copies[2].wait()
    up_pre = dot(rows_ref[:, :model], up_ref[...])
    copies[3].wait()
    hidden_grad = dot_nt(rows_ref[:, model:], down_ref[...])
    sigmoid = jax.nn.sigmoid(gate_pre)
    slope = sigmoid * (1.0 + gate_pre * (1.0 - sigmoid))
    gate_grad = (hidden_grad * up_pre * slope).astype(jnp.bfloat16)
    up_grad = (hidden_grad * gate_pre * sigmoid).astype(jnp.bfloat16)
    gate_grad_ref[...] = gate_grad
    up_grad_ref[...] = up_grad
    along = jnp.sum(
        gate_grad.astype(jnp.float32) * gate_pre + up_grad.astype(jnp.float32) * up_pre,
        -1,
        keepdims=True,
    )
    part = dot_nt(gate_grad, gate_ref[:front, :]) + dot_nt(up_grad, up_ref[:front, :])
    front_ref[:, :front] = part.astype(jnp.bfloat16)
    whole = jnp.broadcast_to(along, (along.shape[0], LANES))
    high = whole.astype(jnp.bfloat16).astype(jnp.float32)
    lane = lax.broadcasted_iota(jnp.int32, whole.shape, 1)
    tail = jnp.where(lane == 0, high, jnp.where(lane == 1, whole - high, 0.0))
    front_ref[:, front:] = tail.astype(jnp.bfloat16)


def expert(rows, gate_mat, up_mat, down_mat, front):
    slots = rows.shape[0]
    model, units = gate_mat.shape
    operands = (rows, gate_mat, up_mat, down_mat)
    return pl.pallas_call(
        functools.partial(expert_kernel, model, front),
        in_specs=[pl.BlockSpec(memory_space=pl.ANY)] * 4,
        out_shape=[
            jax.ShapeDtypeStruct((slots, front + LANES), jnp.bfloat16),
            jax.ShapeDtypeStruct((slots, units), jnp.bfloat16),
            jax.ShapeDtypeStruct((slots, units), jnp.bfloat16),
        ],
        scratch_shapes=[pltpu.VMEM(x.shape, x.dtype) for x in operands]
        + [pltpu.SemaphoreType.DMA((4,))],
        compiler_params=params(60),
        cost_estimate=pl.CostEstimate(
            flops=2 * slots * units * (3 * model + 2 * front),
            bytes_accessed=6 * model * units + 4 * slots * model,
            transcendentals=slots * units,
        ),
        name="expert_rows",
    )(*operands)


def second_kernel(gate_grad_ref, up_grad_ref, gate_ref, up_ref, second_ref):
    second_ref[...] = (
        dot_nt(gate_grad_ref[...], gate_ref[...]) + dot_nt(up_grad_ref[...], up_ref[...])
    ).astype(jnp.bfloat16)


def second_rows(gate_grad, up_grad, gate_mat, up_mat, front):
    slots, units = gate_grad.shape
    width = 512
    rest = gate_mat.shape[0] - front
    whole = pl.BlockSpec((slots, units), lambda i: (0, 0))
    mat = pl.BlockSpec((width, units), lambda i: (front // width + i, 0))
    return pl.pallas_call(
        second_kernel,
        grid=(rest // width,),
        in_specs=[whole, whole, mat, mat],
        out_specs=pl.BlockSpec((slots, width), lambda i: (0, i)),
        out_shape=jax.ShapeDtypeStruct((slots, rest), jnp.bfloat16),
        compiler_params=params(60),
        cost_estimate=pl.CostEstimate(
            flops=4 * slots * units * rest, bytes_accessed=4 * rest * units, transcendentals=0
        ),
        name="second_rows",
    )(gate_grad, up_grad, gate_mat, up_mat)


NEAR = ((0, 0), (0, 1), (3, 0), (1, 0))
FAR = ((2, 0), (1, 1), (3, 1), (2, 1))


def source_of(ctx, place):
    chip = lax.div(ctx, 2)
    x = lax.rem(lax.div(chip, 2) + place[0], 4)
    y = lax.rem(lax.rem(chip, 2) + place[1], 2)
    return 2 * x + y


def ids_in_order(ctx, every_ref):
    core = lax.rem(ctx, 2)
    parts = [every_ref[2 * source_of(ctx, place) + core] for place in NEAR + FAR]
    parts += [every_ref[2 * source_of(ctx, place) + 1 - core] for place in NEAR + FAR]
    return jnp.concatenate(parts, 1).astype(jnp.float32)


def attend_kernel(scale, heads, pieces, ctx_ref, query_ref, every_ref, *refs):
    number = sum(pieces)
    own_refs, other_refs, refs = refs[:number], refs[number : 2 * number], refs[2 * number :]
    out_ref, attend_ref, row_ref, key_ref, value_ref, far_key_ref, far_value_ref = refs[:7]
    here_scr, every_scr = refs[7:]
    rows = query_ref.shape[0]

    @pl.when(pl.program_id(0) == 0)
    def _():
        here_scr[...] = column_of(every_ref[ctx_ref[0]])
        every_scr[...] = ids_in_order(ctx_ref[0], every_ref)

    allowed = here_scr[:, :1] == every_scr[...]
    for h in range(heads):
        columns = slice(h * HEAD_DIM, (h + 1) * HEAD_DIM)
        for blocks, outs in (
            (own_refs, (key_ref, value_ref)), (other_refs, (far_key_ref, far_value_ref))
        ):
            for place, count in enumerate(pieces):
                start = sum(pieces[:place])
                for which, out in enumerate(outs):
                    if count == 1:
                        part = blocks[start][which * rows : (which + 1) * rows, columns]
                    else:
                        part = blocks[start + which][:, columns]
                    out[h, place * rows : (place + 1) * rows, :] = part
        key = jnp.concatenate([key_ref[h], far_key_ref[h]], 0)
        value = jnp.concatenate([value_ref[h], far_value_ref[h]], 0)
        scores = jnp.where(allowed, dot_nt(query_ref[:, columns], key) * scale, MASKED)
        peak = jnp.max(scores, -1, keepdims=True)
        attend = jnp.where(allowed, jnp.exp(scores - peak), 0.0)
        summed = jnp.sum(attend, -1, keepdims=True)
        attend = (attend * (1.0 / summed)).astype(jnp.bfloat16)
        attend_ref[h] = attend
        out_ref[:, columns] = dot(attend, value)
        lse = jnp.broadcast_to(peak + jnp.log(summed), here_scr.shape)
        row_ref[h] = lse.T[:8, :]


def attend_own(ctx, query, every, pieces, own_blocks, other_blocks, heads):
    rows, front = query.shape
    n_ctx = every.shape[0]
    count = n_ctx * rows
    each = 2
    own = pl.BlockSpec((rows, each * HEAD_DIM), lambda h, ctx: (0, h))
    half = pl.BlockSpec((each, count // 2, HEAD_DIM), lambda h, ctx: (h, 0, 0))
    blocks = (*own_blocks, *other_blocks)
    return pl.pallas_call(
        functools.partial(attend_kernel, HEAD_DIM ** (-0.5), each, pieces),
        grid_spec=pltpu.PrefetchScalarGridSpec(
            num_scalar_prefetch=1,
            grid=(heads // each,),
            in_specs=[own, pl.BlockSpec((n_ctx, 1, rows), lambda h, ctx: (0, 0, 0))]
            + [
                pl.BlockSpec((block.shape[0], each * HEAD_DIM), lambda h, ctx: (0, h))
                for block in blocks
            ],
            out_specs=[
                own,
                pl.BlockSpec((each, rows, count), lambda h, ctx: (h, 0, 0)),
                pl.BlockSpec((each, 8, rows), lambda h, ctx: (h, 0, 0)),
            ]
            + [half] * 4,
            scratch_shapes=[
                pltpu.VMEM((rows, LANES), jnp.float32),
                pltpu.VMEM((1, count), jnp.float32),
            ],
        ),
        out_shape=[
            jax.ShapeDtypeStruct((rows, front), jnp.float32),
            jax.ShapeDtypeStruct((heads, rows, count), jnp.bfloat16),
            jax.ShapeDtypeStruct((heads, 8, rows), jnp.float32),
        ]
        + [jax.ShapeDtypeStruct((heads, count // 2, HEAD_DIM), jnp.bfloat16)] * 4,
        compiler_params=params(60),
        cost_estimate=pl.CostEstimate(
            flops=4 * rows * count * front,
            bytes_accessed=8 * count * front,
            transcendentals=rows * count * heads,
        ),
        name="attend_own",
    )(ctx, query, every, *blocks)


def front_kernel(
    model, heads,
    returned_ref, back_ref, hidden_ref, out_grad_ref, gain_ref, inverse_ref, out_ref, lse_ref,
    grad_ref, delta_ref, along_ref, residual_ref,
):
    front = heads * HEAD_DIM
    rows = hidden_ref.shape[0]
    inverse = inverse_ref[:, :1]
    sums = dot(back_ref[...], returned_ref[...])
    along = jnp.sum(sums[:, front:], -1, keepdims=True) * (1.0 / model)
    along_ref[...] = jnp.broadcast_to(along, along_ref.shape)
    weighted = gain_ref[...] * sums[:, :front]
    hidden = hidden_ref[...].astype(jnp.float32)
    residual = out_grad_ref[...].astype(jnp.float32) + inverse * weighted
    residual = residual - hidden * (inverse * inverse * along)
    grad = residual.astype(jnp.bfloat16)
    grad_ref[:rows, :] = grad
    residual_ref[...] = grad
    product = grad.astype(jnp.float32) * out_ref[...]
    pad = jnp.zeros((grad_ref.shape[0] - rows - 6, rows), jnp.bfloat16)
    for h in range(heads):
        columns = slice(h * HEAD_DIM, (h + 1) * HEAD_DIM)
        delta = jnp.broadcast_to(jnp.sum(product[:, columns], -1, keepdims=True), (rows, rows))
        delta_ref[:, columns] = delta
        parts = three_parts(delta.T[:1, :]) + three_parts(lse_ref[h][:1, :])
        parts = [part.astype(jnp.float32) for part in parts] + [pad.astype(jnp.float32)]
        grad_ref[rows:, columns] = jnp.concatenate(parts, 0).astype(jnp.bfloat16)


def front_grad(returned, back, hidden, out_grad, gain, inverse, out, lse_rows, heads):
    rows, model = hidden.shape
    slots = back.shape[1]
    front = heads * HEAD_DIM
    extra = 16
    whole = lambda shape: pl.BlockSpec(shape, lambda i: (0,) * len(shape))
    return pl.pallas_call(
        functools.partial(front_kernel, model, heads),
        grid=(1,),
        in_specs=[
            whole((slots, front + LANES)),
            whole((rows, slots)),
            whole((rows, front)),
            whole((rows, front)),
            whole((1, front)),
            whole((rows, LANES)),
            whole((rows, front)),
            whole((heads, 8, rows)),
        ],
        out_specs=[
            whole((rows + extra, front)),
            whole((rows, front)),
            whole((rows, LANES)),
            whole((rows, front)),
        ],
        out_shape=[
            jax.ShapeDtypeStruct((rows + extra, front), jnp.bfloat16),
            jax.ShapeDtypeStruct((rows, front), jnp.float32),
            jax.ShapeDtypeStruct((rows, LANES), jnp.float32),
            jax.ShapeDtypeStruct((rows, model), jnp.bfloat16),
        ],
        compiler_params=params(60),
        cost_estimate=pl.CostEstimate(
            flops=2 * slots * rows * front, bytes_accessed=6 * slots * front, transcendentals=0
        ),
        name="front_grad",
    )(returned, back, hidden, out_grad, gain, inverse, out, lse_rows)


def rest_kernel(
    returned_ref, back_ref, hidden_ref, out_grad_ref, gain_ref, inverse_ref, along_ref, _,
    residual_ref,
):
    inverse = inverse_ref[:, :1]
    weighted = gain_ref[...] * dot(back_ref[...], returned_ref[...])
    hidden = hidden_ref[...].astype(jnp.float32)
    residual = out_grad_ref[...].astype(jnp.float32) + inverse * weighted
    residual = residual - hidden * (inverse * inverse * along_ref[:, :1])
    residual_ref[...] = residual.astype(jnp.bfloat16)


def rest_grad(returned, back, hidden, out_grad, gain, inverse, along, residual):
    rows, model = hidden.shape
    slots, rest = returned.shape
    whole = lambda shape: pl.BlockSpec(shape, lambda i: (0,) * len(shape))
    second = pl.BlockSpec((rows, rest), lambda i: (0, 1))
    return pl.pallas_call(
        rest_kernel,
        grid=(1,),
        in_specs=[
            whole((slots, rest)),
            whole((rows, slots)),
            second,
            second,
            pl.BlockSpec((1, rest), lambda i: (0, 1)),
            whole((rows, LANES)),
            whole((rows, LANES)),
            pl.BlockSpec(memory_space=pl.ANY),
        ],
        out_specs=second,
        out_shape=jax.ShapeDtypeStruct((rows, model), jnp.bfloat16),
        input_output_aliases={7: 0},
        compiler_params=params(60),
        cost_estimate=pl.CostEstimate(
            flops=2 * slots * rows * rest, bytes_accessed=8 * rows * model, transcendentals=0
        ),
        name="rest_grad",
    )(returned, back, hidden, out_grad, gain, inverse, along, residual)


def query_kernel(
    scale, heads,
    grad_ref, attend_ref, key_ref, value_ref, far_key_ref, far_value_ref, delta_ref, *refs
):
    result_ref = refs[-1]
    for h in range(heads):
        columns = slice(h * HEAD_DIM, (h + 1) * HEAD_DIM)
        key = jnp.concatenate([key_ref[h], far_key_ref[h]], 0)
        value = jnp.concatenate([value_ref[h], far_value_ref[h]], 0)
        attend_grad = dot_nt(grad_ref[:, columns], value)
        delta = delta_ref[:, columns][:, :1]
        score_grad = attend_ref[h].astype(jnp.float32) * (attend_grad - delta)
        result_ref[:, columns] = (dot(score_grad.astype(jnp.bfloat16), key) * scale).astype(
            jnp.bfloat16
        )


def query_grads(grad, attend, key, value, far_key, far_value, delta, first, heads, before):
    total, rows, count = attend.shape
    each = 2
    skip = first // each
    own = pl.BlockSpec((rows, each * HEAD_DIM), lambda h: (0, skip + h))
    half = pl.BlockSpec((each, count // 2, HEAD_DIM), lambda h: (skip + h, 0, 0))
    return pl.pallas_call(
        functools.partial(query_kernel, HEAD_DIM ** (-0.5), each),
        grid=(heads // each,),
        in_specs=[own, pl.BlockSpec((each, rows, count), lambda h: (skip + h, 0, 0))]
        + [half] * 4
        + [own]
        + [pl.BlockSpec(memory_space=pl.ANY)] * len(before),
        out_specs=own,
        out_shape=jax.ShapeDtypeStruct((rows, total * HEAD_DIM), jnp.bfloat16),
        input_output_aliases={7: 0} if before else {},
        compiler_params=params(60),
        cost_estimate=pl.CostEstimate(
            flops=4 * rows * count * heads * HEAD_DIM,
            bytes_accessed=6 * count * heads * HEAD_DIM,
            transcendentals=0,
        ),
        name="query_grads",
    )(grad, attend, key, value, far_key, far_value, delta, *before)


def key_kernel(
    scale, heads, places, pieces, query_pieces, last,
    ctx_ref, key_ref, value_ref, far_key_ref, far_value_ref, every_ref, *refs
):
    query_refs, refs = refs[: sum(query_pieces)], refs[sum(query_pieces) :]
    grad_refs, refs = refs[: sum(pieces)], refs[sum(pieces) :]
    rows = key_ref.shape[1]
    ctx = ctx_ref[0]
    core = lax.rem(ctx, 2)
    chip = lax.div(ctx, 2)
    here_scr, refs = refs[-1], refs[:-1]

    @pl.when(pl.program_id(0) == 0)
    def _():
        here_scr[:rows, :] = column_of(every_ref[ctx])
        here_scr[rows:, :] = column_of(every_ref[2 * chip + 1 - core])

    here = here_scr[:, :1]
    parts, every = [], []
    for i, place in enumerate(places):
        start = sum(pieces[:i])
        parts.append(
            jnp.concatenate([ref[...] for ref in grad_refs[start : start + pieces[i]]], 0)
        )
        every.append(every_ref[2 * source_of(ctx, place) + core])
    extra = jnp.concatenate([part[rows:] for part in parts], 1).astype(jnp.float32)
    delta = extra[0:1] + extra[1:2] + extra[2:3]
    lse = extra[3:4] + extra[4:5] + extra[5:6]
    allowed = here == jnp.concatenate(every, 1).astype(jnp.float32)
    width = parts[0].shape[1]
    for h in range(heads):
        columns = slice(h * HEAD_DIM, (h + 1) * HEAD_DIM)

        def lanes(row):
            starts = [i * width + h * HEAD_DIM for i in range(len(places))]
            return jnp.concatenate([row[:, i : i + HEAD_DIM] for i in starts], 1)

        key = jnp.concatenate([key_ref[h], far_key_ref[h]], 0)
        value = jnp.concatenate([value_ref[h], far_value_ref[h]], 0)
        query = jnp.concatenate([ref[:, columns] for ref in query_refs], 0)
        grad = jnp.concatenate([part[:rows, columns] for part in parts], 0)
        scores = dot_nt(key, query) * scale
        attend = jnp.where(allowed, jnp.exp(scores - lanes(lse)), 0.0)
        score_grad = attend * (dot_nt(value, grad) - lanes(delta))
        value_part = dot(attend.astype(jnp.bfloat16), grad)
        key_part = dot(score_grad.astype(jnp.bfloat16), query)
        if last:
            key_in, value_in, own_ref, other_ref = refs
            key_part = (key_in[h] + key_part) * scale
            value_part = value_in[h] + value_part
            own_ref[0, h] = key_part[:rows].astype(jnp.bfloat16)
            own_ref[1, h] = value_part[:rows].astype(jnp.bfloat16)
            other_ref[0, h] = key_part[rows:].astype(jnp.bfloat16)
            other_ref[1, h] = value_part[rows:].astype(jnp.bfloat16)
        else:
            key_out, value_out = refs
            key_out[h] = key_part
            value_out[h] = value_part


def key_grads(
    ctx, key, value, far_key, far_value, every, query_pieces, queries, pieces, grads, sums
):
    heads = key.shape[0]
    n_ctx, _, rows = every.shape
    last = sums is not None
    each = 2
    width = each * HEAD_DIM
    places = FAR if last else NEAR
    counted = len(places) * rows
    mine = pl.BlockSpec((each, rows, HEAD_DIM), lambda h, ctx: (h, 0, 0))
    piece_specs = [
        pl.BlockSpec((piece.shape[0], width), lambda h, ctx: (0, h)) for piece in (*queries, *grads)
    ]
    sum_spec = pl.BlockSpec((each, 2 * rows, HEAD_DIM), lambda h, ctx: (h, 0, 0))
    pair_spec = pl.BlockSpec((2, each, rows, HEAD_DIM), lambda h, ctx: (0, h, 0, 0))
    sum_shape = (heads, 2 * rows, HEAD_DIM)
    pair_shape = (2, heads, rows, HEAD_DIM)
    here = [pltpu.VMEM((2 * rows, LANES), jnp.float32)]
    if last:
        extra_in = [sum_spec, sum_spec]
        out_specs = [pair_spec, pair_spec]
        out_shape = [jax.ShapeDtypeStruct(pair_shape, jnp.bfloat16)] * 2
    else:
        extra_in = []
        out_specs = [sum_spec, sum_spec]
        out_shape = [jax.ShapeDtypeStruct(sum_shape, jnp.float32)] * 2
    return pl.pallas_call(
        functools.partial(
            key_kernel, HEAD_DIM ** (-0.5), each, places, pieces, query_pieces, last
        ),
        grid_spec=pltpu.PrefetchScalarGridSpec(
            num_scalar_prefetch=1,
            grid=(heads // each,),
            in_specs=[mine] * 4
            + [
                pl.BlockSpec((n_ctx, 1, rows), lambda h, ctx: (0, 0, 0)),
            ]
            + piece_specs
            + extra_in,
            out_specs=out_specs,
            scratch_shapes=here,
        ),
        out_shape=out_shape,
        compiler_params=params(60),
        cost_estimate=pl.CostEstimate(
            flops=16 * rows * counted * heads * HEAD_DIM,
            bytes_accessed=8 * counted * heads * HEAD_DIM,
            transcendentals=2 * rows * counted * heads,
        ),
        name="key_grads_last" if last else "key_grads_first",
    )(ctx, key, value, far_key, far_value, every, *queries, *grads, *(sums or ()))


def finish_kernel(own_ref, arrived_ref, key_ref, value_ref):
    total = own_ref[...].astype(jnp.float32) + arrived_ref[...].astype(jnp.float32)
    for h in range(own_ref.shape[1]):
        columns = slice(h * HEAD_DIM, (h + 1) * HEAD_DIM)
        key_ref[:, columns] = total[0, h].astype(jnp.bfloat16)
        value_ref[:, columns] = total[1, h].astype(jnp.bfloat16)


def finish(own, arrived):
    _, heads, rows, size = own.shape
    each = 4
    pair = pl.BlockSpec((2, each, rows, size), lambda h: (0, h, 0, 0))
    return pl.pallas_call(
        finish_kernel,
        grid=(heads // each,),
        in_specs=[pair, pair],
        out_specs=[pl.BlockSpec((rows, each * size), lambda h: (0, h))] * 2,
        out_shape=[jax.ShapeDtypeStruct((rows, heads * size), jnp.bfloat16)] * 2,
        compiler_params=params(60),
        name="finish",
    )(own, arrived)


def body(
    queries, keys, values, segments, hidden_state, norm_gain,
    route_gates, routes, out_grad, w_gate, w_up, w_down,
):
    rows, model = hidden_state.shape[1:]
    front = queries.shape[2]
    heads = front // HEAD_DIM
    n_exp = lax.axis_size("exp")
    capacity = 3 * rows * TOP // (2 * n_exp)
    hidden, grad_in = hidden_state[0], out_grad[0]
    gain = norm_gain[None, :]
    query, key, value = queries[0], keys[0], values[0]
    gate_mat, up_mat, down_mat = w_gate[0], w_up[0], w_down[0]
    n_ctx = lax.axis_size("ctx")
    ctx = lax.axis_index("ctx")[None]
    every = segments[0].reshape(n_ctx, 1, rows)

    def exchange(x):
        cut = x.reshape(n_exp, capacity, x.shape[1])
        return lax.all_to_all(cut, "exp", split_axis=0, concat_axis=0, tiled=True).reshape(x.shape)

    def right(x):
        return lax.ppermute(x, "ctx", [(i, (i + 4) % n_ctx) for i in range(n_ctx)])

    def left(x):
        return lax.ppermute(x, "ctx", [(i, (i - 4) % n_ctx) for i in range(n_ctx)])

    def across(x):
        return lax.ppermute(x, "ctx", [(i, i ^ 2) for i in range(n_ctx)])

    def swap_core(x):
        return lax.ppermute(x, "ctx", [(i, i ^ 1) for i in range(n_ctx)])

    def first_round(x):
        return across(x), right(x), left(x)

    def second_round(from_y, from_left, from_right):
        return right(from_left), left(from_y), across(from_left)

    def third_round(far, y_right, y_left):
        cut = far.shape[0] // 3
        return across(far[:cut]), left(y_right[cut : 2 * cut]), right(y_left[2 * cut :])

    send, back, inverse = pack(
        routes[0].T, route_gates[0].T, hidden, gain, grad_in, n_exp, capacity
    )
    def spread(x, near):
        half = x.shape[0] // 2
        from_y, from_left, from_right = near
        far = (right(from_left[:half]), left(from_right[half:]))
        return (x, *near, *far, left(from_y), right(from_y))

    def spread_last(parts):
        y_right, y_left = parts[-2:]
        half = y_right.shape[0] // 2
        return (*parts, right(y_left[:half]), left(y_right[half:]))

    pieces = (1, 1, 1, 1, 2, 1, 1, 2)
    key, value, query, inverse = lax.optimization_barrier((key, value, query, inverse))
    arrived = exchange(send)
    stacked = jnp.concatenate([key, value], 0)
    parts = spread(stacked, first_round(stacked))
    query_then, *parts = lax.optimization_barrier((query, *parts))
    blocks = spread_last(parts)
    other_blocks = [swap_core(block) for block in blocks]
    query_near = first_round(query_then)
    number = len(blocks)
    arrived, *all_blocks = lax.optimization_barrier(
        (arrived, *blocks, *other_blocks, *query_near)
    )
    blocks, other_blocks = all_blocks[:number], all_blocks[number : 2 * number]
    query_near = all_blocks[2 * number :]
    first, gate_grad, up_grad = expert(arrived, gate_mat, up_mat, down_mat, front)
    first = exchange(first)
    query, gate_grad = lax.optimization_barrier((query, gate_grad))
    query_parts = spread(query, query_near)
    second = second_rows(gate_grad, up_grad, gate_mat, up_mat, front)
    out, attend, lse_rows, *held = attend_own(
        ctx, query, every, pieces, blocks, other_blocks, heads
    )
    out, *query_parts = lax.optimization_barrier((out, *query_parts))
    query_parts = spread_last(query_parts)
    first, second, *query_parts = lax.optimization_barrier((first, second, *query_parts))
    grad, delta, along, residual = front_grad(
        first, back, hidden, grad_in, gain, inverse, out, lse_rows, heads
    )
    near = first_round(grad)
    half = heads // 2
    query_front = query_grads(grad, attend, *held, delta, 0, half, ())
    grad_then, query_front, *near = lax.optimization_barrier((grad, query_front, *near))
    far = second_round(*near)
    query_grad = query_grads(
        grad_then, attend, *held, delta, half, half, (query_front,)
    )
    held_back = lax.optimization_barrier((second, query_grad, *far, grad_then, *near))
    second, query_grad, far, near = held_back[0], held_back[1], held_back[2:5], held_back[5:]
    second = exchange(second)
    last = third_round(*far)
    sums = key_grads(
        ctx, *held, every, (1,) * 4, query_parts[:4], (1,) * 4, tuple(near), None
    )
    own, other = key_grads(
        ctx, *held, every, (2, 1, 1, 2), query_parts[4:], (1, 1, 1, 3), (*far, *last), sums
    )
    other = swap_core(other)
    residual_grad = rest_grad(second, back, hidden, grad_in, gain, inverse, along, residual)
    other, residual_grad = lax.optimization_barrier((other, residual_grad))
    key_grad, value_grad = finish(own, other)
    return (query_grad[None], key_grad[None], value_grad[None], residual_grad[None])


def solution(mesh):
    rows = P("exp", "ctx", None)
    mats = P("exp", None, None)
    in_specs = (rows, rows, rows, P("exp", None), rows, P(), rows, rows, rows, mats, mats, mats)
    return jax.shard_map(
        body, mesh=mesh, in_specs=in_specs, out_specs=(rows,) * 4, check_vma=False
    )
```

```python
import functools

import jax
import jax.numpy as jnp
from jax import lax
from jax.experimental import pallas as pl
from jax.experimental.pallas import tpu as pltpu
from jax.sharding import PartitionSpec as P

HEAD_DIM = 128
TOP = 2
EPSILON = 1e-06
MASKED = -1e30
LANES = 128
NT = (((1,), (1,)), ((), ()))
MIB = 1 << 20
VMEM = pltpu.MemorySpace.VMEM


def params(limit_mib, **more):
    return pltpu.CompilerParams(vmem_limit_bytes=limit_mib * MIB, **more)


def dot(a, b):
    return jnp.dot(a, b, preferred_element_type=jnp.float32)


def dot_nt(a, b):
    return lax.dot_general(a, b, NT, preferred_element_type=jnp.float32)


def three_parts(x):
    high = x.astype(jnp.bfloat16)
    rest = x - high.astype(jnp.float32)
    mid = rest.astype(jnp.bfloat16)
    low = (rest - mid.astype(jnp.float32)).astype(jnp.bfloat16)
    return high, mid, low


def column_of(row):
    size = row.shape[1]
    return jnp.broadcast_to(row.astype(jnp.float32), (size, size)).T


def pack_kernel(
    n_exp, capacity, block,
    routes_ref, gates_ref, hidden_ref, gain_ref, out_grad_ref,
    send_ref, back_ref, inverse_ref,
    rows_scr, pick_scr,
):
    step = pl.program_id(0)
    rows, model = hidden_ref.shape
    slots = n_exp * capacity

    @pl.when(step == 0)
    def _():
        hidden = hidden_ref[...].astype(jnp.float32)
        inverse = lax.rsqrt(jnp.mean(hidden * hidden, -1, keepdims=True) + EPSILON)
        inverse_ref[...] = jnp.broadcast_to(inverse, inverse_ref.shape)
        normed = (hidden * inverse * gain_ref[...]).astype(jnp.bfloat16)
        out_grad = out_grad_ref[...].astype(jnp.float32)
        expert_id = lax.broadcasted_iota(jnp.int32, (n_exp, rows), 0)
        earlier = (
            lax.broadcasted_iota(jnp.int32, (rows, rows), 0)
            < lax.broadcasted_iota(jnp.int32, (rows, rows), 1)
        ).astype(jnp.bfloat16)
        slot_id = lax.broadcasted_iota(jnp.int32, (slots, rows), 0).astype(jnp.float32)
        first_slot = expert_id.astype(jnp.float32) * capacity
        total = None
        for j in range(TOP):
            part = slice(j * rows, (j + 1) * rows)
            named = (expert_id == routes_ref[j : j + 1, :]).astype(jnp.float32)
            place = first_slot + dot(named.astype(jnp.bfloat16), earlier)
            if j:
                place = place + used
            target = jnp.sum(named * place, 0, keepdims=True)
            pick = (slot_id == target).astype(jnp.float32)
            pick_scr[:, part] = pick.astype(jnp.bfloat16)
            total = pick if total is None else total + pick
            if j == 0:
                used = jnp.sum(named, 1, keepdims=True)
            gate = jnp.broadcast_to(gates_ref[j : j + 1, :], (rows, rows)).T[:, :1]
            rows_scr[part, :model] = normed
            rows_scr[part, model:] = (gate * out_grad).astype(jnp.bfloat16)
        back_ref[...] = total.T.astype(jnp.bfloat16)

    pick = pick_scr[pl.ds(pl.multiple_of(step * block, block), block), :]
    send_ref[...] = dot(pick, rows_scr[...]).astype(jnp.bfloat16)


def pack(routes_t, gates_t, hidden, gain, out_grad, n_exp, capacity):
    rows, model = hidden.shape
    slots = n_exp * capacity
    block = slots // 2
    whole = lambda shape: pl.BlockSpec(shape, lambda i: (0,) * len(shape))
    return pl.pallas_call(
        functools.partial(pack_kernel, n_exp, capacity, block),
        grid=(slots // block,),
        in_specs=[
            whole((TOP, rows)),
            whole((TOP, rows)),
            whole((rows, model)),
            whole((1, model)),
            whole((rows, model)),
        ],
        out_specs=[
            pl.BlockSpec((block, 2 * model), lambda i: (i, 0)),
            whole((rows, slots)),
            whole((rows, LANES)),
        ],
        out_shape=[
            jax.ShapeDtypeStruct((slots, 2 * model), jnp.bfloat16),
            jax.ShapeDtypeStruct((rows, slots), jnp.bfloat16),
            jax.ShapeDtypeStruct((rows, LANES), jnp.float32),
        ],
        scratch_shapes=[
            pltpu.VMEM((TOP * rows, 2 * model), jnp.bfloat16),
            pltpu.VMEM((slots, TOP * rows), jnp.bfloat16),
        ],
        compiler_params=params(60),
        cost_estimate=pl.CostEstimate(
            flops=8 * slots * rows * model, bytes_accessed=8 * slots * model, transcendentals=0
        ),
        name="pack_rows",
    )(routes_t, gates_t, hidden, gain, out_grad)


def expert_kernel(
    model, front,
    rows_in, gate_in, up_in, down_in,
    front_ref, gate_grad_ref, up_grad_ref,
    rows_ref, gate_ref, up_ref, down_ref, sems,
):
    copies = [
        pltpu.make_async_copy(source, target, sems.at[i])
        for i, (source, target) in enumerate(
            ((rows_in, rows_ref), (gate_in, gate_ref), (up_in, up_ref), (down_in, down_ref))
        )
    ]
    for copy in copies:
        copy.start()
    copies[0].wait()
    copies[1].wait()
    gate_pre = dot(rows_ref[:, :model], gate_ref[...])
    copies[2].wait()
    up_pre = dot(rows_ref[:, :model], up_ref[...])
    copies[3].wait()
    hidden_grad = dot_nt(rows_ref[:, model:], down_ref[...])
    sigmoid = jax.nn.sigmoid(gate_pre)
    slope = sigmoid * (1.0 + gate_pre * (1.0 - sigmoid))
    gate_grad = (hidden_grad * up_pre * slope).astype(jnp.bfloat16)
    up_grad = (hidden_grad * gate_pre * sigmoid).astype(jnp.bfloat16)
    gate_grad_ref[...] = gate_grad
    up_grad_ref[...] = up_grad
    along = jnp.sum(
        gate_grad.astype(jnp.float32) * gate_pre + up_grad.astype(jnp.float32) * up_pre,
        -1,
        keepdims=True,
    )
    part = dot_nt(gate_grad, gate_ref[:front, :]) + dot_nt(up_grad, up_ref[:front, :])
    front_ref[:, :front] = part.astype(jnp.bfloat16)
    whole = jnp.broadcast_to(along, (along.shape[0], LANES))
    high = whole.astype(jnp.bfloat16).astype(jnp.float32)
    lane = lax.broadcasted_iota(jnp.int32, whole.shape, 1)
    tail = jnp.where(lane == 0, high, jnp.where(lane == 1, whole - high, 0.0))
    front_ref[:, front:] = tail.astype(jnp.bfloat16)


def expert(rows, gate_mat, up_mat, down_mat, front):
    slots = rows.shape[0]
    model, units = gate_mat.shape
    operands = (rows, gate_mat, up_mat, down_mat)
    return pl.pallas_call(
        functools.partial(expert_kernel, model, front),
        in_specs=[pl.BlockSpec(memory_space=pl.ANY)] * 4,
        out_shape=[
            jax.ShapeDtypeStruct((slots, front + LANES), jnp.bfloat16),
            jax.ShapeDtypeStruct((slots, units), jnp.bfloat16),
            jax.ShapeDtypeStruct((slots, units), jnp.bfloat16),
        ],
        scratch_shapes=[pltpu.VMEM(x.shape, x.dtype) for x in operands]
        + [pltpu.SemaphoreType.DMA((4,))],
        compiler_params=params(60),
        cost_estimate=pl.CostEstimate(
            flops=2 * slots * units * (3 * model + 2 * front),
            bytes_accessed=6 * model * units + 4 * slots * model,
            transcendentals=slots * units,
        ),
        name="expert_rows",
    )(*operands)


def second_kernel(gate_grad_ref, up_grad_ref, gate_ref, up_ref, second_ref):
    second_ref[...] = (
        dot_nt(gate_grad_ref[...], gate_ref[...]) + dot_nt(up_grad_ref[...], up_ref[...])
    ).astype(jnp.bfloat16)


def second_rows(gate_grad, up_grad, gate_mat, up_mat, front):
    slots, units = gate_grad.shape
    width = 512
    rest = gate_mat.shape[0] - front
    whole = pl.BlockSpec((slots, units), lambda i: (0, 0))
    mat = pl.BlockSpec((width, units), lambda i: (front // width + i, 0))
    return pl.pallas_call(
        second_kernel,
        grid=(rest // width,),
        in_specs=[whole, whole, mat, mat],
        out_specs=pl.BlockSpec((slots, width), lambda i: (0, i)),
        out_shape=jax.ShapeDtypeStruct((slots, rest), jnp.bfloat16),
        compiler_params=params(60),
        cost_estimate=pl.CostEstimate(
            flops=4 * slots * units * rest, bytes_accessed=4 * rest * units, transcendentals=0
        ),
        name="second_rows",
    )(gate_grad, up_grad, gate_mat, up_mat)


NEAR = ((0, 0), (0, 1), (3, 0), (1, 0))
FAR = ((2, 0), (1, 1), (3, 1), (2, 1))


def source_of(ctx, place):
    chip = lax.div(ctx, 2)
    x = lax.rem(lax.div(chip, 2) + place[0], 4)
    y = lax.rem(lax.rem(chip, 2) + place[1], 2)
    return 2 * x + y


def ids_in_order(ctx, every_ref):
    core = lax.rem(ctx, 2)
    parts = [every_ref[2 * source_of(ctx, place) + core] for place in NEAR + FAR]
    parts += [every_ref[2 * source_of(ctx, place) + 1 - core] for place in NEAR + FAR]
    return jnp.concatenate(parts, 1).astype(jnp.float32)


def attend_kernel(scale, heads, pieces, ctx_ref, query_ref, every_ref, *refs):
    number = sum(pieces)
    own_refs, other_refs, refs = refs[:number], refs[number : 2 * number], refs[2 * number :]
    out_ref, attend_ref, row_ref, key_ref, value_ref, far_key_ref, far_value_ref = refs[:7]
    here_scr, every_scr = refs[7:]
    rows = query_ref.shape[0]

    @pl.when(pl.program_id(0) == 0)
    def _():
        here_scr[...] = column_of(every_ref[ctx_ref[0]])
        every_scr[...] = ids_in_order(ctx_ref[0], every_ref)

    allowed = here_scr[:, :1] == every_scr[...]
    for h in range(heads):
        columns = slice(h * HEAD_DIM, (h + 1) * HEAD_DIM)
        for blocks, outs in (
            (own_refs, (key_ref, value_ref)), (other_refs, (far_key_ref, far_value_ref))
        ):
            for place, count in enumerate(pieces):
                start = sum(pieces[:place])
                for which, out in enumerate(outs):
                    if count == 1:
                        part = blocks[start][which * rows : (which + 1) * rows, columns]
                    else:
                        part = blocks[start + which][:, columns]
                    out[h, place * rows : (place + 1) * rows, :] = part
        key = jnp.concatenate([key_ref[h], far_key_ref[h]], 0)
        value = jnp.concatenate([value_ref[h], far_value_ref[h]], 0)
        scores = jnp.where(allowed, dot_nt(query_ref[:, columns], key) * scale, MASKED)
        peak = jnp.max(scores, -1, keepdims=True)
        attend = jnp.where(allowed, jnp.exp(scores - peak), 0.0)
        summed = jnp.sum(attend, -1, keepdims=True)
        attend = (attend * (1.0 / summed)).astype(jnp.bfloat16)
        attend_ref[h] = attend
        out_ref[:, columns] = dot(attend, value)
        lse = jnp.broadcast_to(peak + jnp.log(summed), here_scr.shape)
        row_ref[h] = lse.T[:8, :]


def attend_own(ctx, query, every, pieces, own_blocks, other_blocks, heads):
    rows, front = query.shape
    n_ctx = every.shape[0]
    count = n_ctx * rows
    each = 2
    own = pl.BlockSpec((rows, each * HEAD_DIM), lambda h, ctx: (0, h))
    half = pl.BlockSpec((each, count // 2, HEAD_DIM), lambda h, ctx: (h, 0, 0))
    blocks = (*own_blocks, *other_blocks)
    return pl.pallas_call(
        functools.partial(attend_kernel, HEAD_DIM ** (-0.5), each, pieces),
        grid_spec=pltpu.PrefetchScalarGridSpec(
            num_scalar_prefetch=1,
            grid=(heads // each,),
            in_specs=[own, pl.BlockSpec((n_ctx, 1, rows), lambda h, ctx: (0, 0, 0))]
            + [
                pl.BlockSpec((block.shape[0], each * HEAD_DIM), lambda h, ctx: (0, h))
                for block in blocks
            ],
            out_specs=[
                own,
                pl.BlockSpec((each, rows, count), lambda h, ctx: (h, 0, 0)),
                pl.BlockSpec((each, 8, rows), lambda h, ctx: (h, 0, 0)),
            ]
            + [half] * 4,
            scratch_shapes=[
                pltpu.VMEM((rows, LANES), jnp.float32),
                pltpu.VMEM((1, count), jnp.float32),
            ],
        ),
        out_shape=[
            jax.ShapeDtypeStruct((rows, front), jnp.float32),
            jax.ShapeDtypeStruct((heads, rows, count), jnp.bfloat16),
            jax.ShapeDtypeStruct((heads, 8, rows), jnp.float32),
        ]
        + [jax.ShapeDtypeStruct((heads, count // 2, HEAD_DIM), jnp.bfloat16)] * 4,
        compiler_params=params(60),
        cost_estimate=pl.CostEstimate(
            flops=4 * rows * count * front,
            bytes_accessed=8 * count * front,
            transcendentals=rows * count * heads,
        ),
        name="attend_own",
    )(ctx, query, every, *blocks)


def front_kernel(
    model, heads,
    returned_ref, back_ref, hidden_ref, out_grad_ref, gain_ref, inverse_ref, out_ref, lse_ref,
    grad_ref, delta_ref, along_ref, residual_ref,
):
    front = heads * HEAD_DIM
    rows = hidden_ref.shape[0]
    inverse = inverse_ref[:, :1]
    sums = dot(back_ref[...], returned_ref[...])
    along = jnp.sum(sums[:, front:], -1, keepdims=True) * (1.0 / model)
    along_ref[...] = jnp.broadcast_to(along, along_ref.shape)
    weighted = gain_ref[...] * sums[:, :front]
    hidden = hidden_ref[...].astype(jnp.float32)
    residual = out_grad_ref[...].astype(jnp.float32) + inverse * weighted
    residual = residual - hidden * (inverse * inverse * along)
    grad = residual.astype(jnp.bfloat16)
    grad_ref[:rows, :] = grad
    residual_ref[...] = grad
    product = grad.astype(jnp.float32) * out_ref[...]
    pad = jnp.zeros((grad_ref.shape[0] - rows - 6, rows), jnp.bfloat16)
    for h in range(heads):
        columns = slice(h * HEAD_DIM, (h + 1) * HEAD_DIM)
        delta = jnp.broadcast_to(jnp.sum(product[:, columns], -1, keepdims=True), (rows, rows))
        delta_ref[:, columns] = delta
        parts = three_parts(delta.T[:1, :]) + three_parts(lse_ref[h][:1, :])
        parts = [part.astype(jnp.float32) for part in parts] + [pad.astype(jnp.float32)]
        grad_ref[rows:, columns] = jnp.concatenate(parts, 0).astype(jnp.bfloat16)


def front_grad(returned, back, hidden, out_grad, gain, inverse, out, lse_rows, heads):
    rows, model = hidden.shape
    slots = back.shape[1]
    front = heads * HEAD_DIM
    extra = 16
    whole = lambda shape: pl.BlockSpec(shape, lambda i: (0,) * len(shape))
    return pl.pallas_call(
        functools.partial(front_kernel, model, heads),
        grid=(1,),
        in_specs=[
            whole((slots, front + LANES)),
            whole((rows, slots)),
            whole((rows, front)),
            whole((rows, front)),
            whole((1, front)),
            whole((rows, LANES)),
            whole((rows, front)),
            whole((heads, 8, rows)),
        ],
        out_specs=[
            whole((rows + extra, front)),
            whole((rows, front)),
            whole((rows, LANES)),
            whole((rows, front)),
        ],
        out_shape=[
            jax.ShapeDtypeStruct((rows + extra, front), jnp.bfloat16),
            jax.ShapeDtypeStruct((rows, front), jnp.float32),
            jax.ShapeDtypeStruct((rows, LANES), jnp.float32),
            jax.ShapeDtypeStruct((rows, model), jnp.bfloat16),
        ],
        compiler_params=params(60),
        cost_estimate=pl.CostEstimate(
            flops=2 * slots * rows * front, bytes_accessed=6 * slots * front, transcendentals=0
        ),
        name="front_grad",
    )(returned, back, hidden, out_grad, gain, inverse, out, lse_rows)


def query_kernel(
    scale, heads,
    grad_ref, attend_ref, key_ref, value_ref, far_key_ref, far_value_ref, delta_ref, *refs
):
    result_ref = refs[-1]
    for h in range(heads):
        columns = slice(h * HEAD_DIM, (h + 1) * HEAD_DIM)
        key = jnp.concatenate([key_ref[h], far_key_ref[h]], 0)
        value = jnp.concatenate([value_ref[h], far_value_ref[h]], 0)
        attend_grad = dot_nt(grad_ref[:, columns], value)
        delta = delta_ref[:, columns][:, :1]
        score_grad = attend_ref[h].astype(jnp.float32) * (attend_grad - delta)
        result_ref[:, columns] = (dot(score_grad.astype(jnp.bfloat16), key) * scale).astype(
            jnp.bfloat16
        )


def query_grads(grad, attend, key, value, far_key, far_value, delta, first, heads, before):
    total, rows, count = attend.shape
    each = 2
    skip = first // each
    own = pl.BlockSpec((rows, each * HEAD_DIM), lambda h: (0, skip + h))
    half = pl.BlockSpec((each, count // 2, HEAD_DIM), lambda h: (skip + h, 0, 0))
    return pl.pallas_call(
        functools.partial(query_kernel, HEAD_DIM ** (-0.5), each),
        grid=(heads // each,),
        in_specs=[own, pl.BlockSpec((each, rows, count), lambda h: (skip + h, 0, 0))]
        + [half] * 4
        + [own]
        + [pl.BlockSpec(memory_space=pl.ANY)] * len(before),
        out_specs=own,
        out_shape=jax.ShapeDtypeStruct((rows, total * HEAD_DIM), jnp.bfloat16),
        input_output_aliases={7: 0} if before else {},
        compiler_params=params(60),
        cost_estimate=pl.CostEstimate(
            flops=4 * rows * count * heads * HEAD_DIM,
            bytes_accessed=6 * count * heads * HEAD_DIM,
            transcendentals=0,
        ),
        name="query_grads",
    )(grad, attend, key, value, far_key, far_value, delta, *before)


def key_kernel(
    scale, heads, places, pieces, query_pieces, last,
    ctx_ref, key_ref, value_ref, far_key_ref, far_value_ref, every_ref, *refs
):
    query_refs, refs = refs[: sum(query_pieces)], refs[sum(query_pieces) :]
    grad_refs, refs = refs[: sum(pieces)], refs[sum(pieces) :]
    rows = key_ref.shape[1]
    ctx = ctx_ref[0]
    core = lax.rem(ctx, 2)
    chip = lax.div(ctx, 2)
    here_scr, refs = refs[-1], refs[:-1]

    @pl.when(pl.program_id(0) == 0)
    def _():
        here_scr[:rows, :] = column_of(every_ref[ctx])
        here_scr[rows:, :] = column_of(every_ref[2 * chip + 1 - core])

    here = here_scr[:, :1]
    parts, every = [], []
    for i, place in enumerate(places):
        start = sum(pieces[:i])
        parts.append(
            jnp.concatenate([ref[...] for ref in grad_refs[start : start + pieces[i]]], 0)
        )
        every.append(every_ref[2 * source_of(ctx, place) + core])
    extra = jnp.concatenate([part[rows:] for part in parts], 1).astype(jnp.float32)
    delta = extra[0:1] + extra[1:2] + extra[2:3]
    lse = extra[3:4] + extra[4:5] + extra[5:6]
    allowed = here == jnp.concatenate(every, 1).astype(jnp.float32)
    width = parts[0].shape[1]
    for h in range(heads):
        columns = slice(h * HEAD_DIM, (h + 1) * HEAD_DIM)

        def lanes(row):
            starts = [i * width + h * HEAD_DIM for i in range(len(places))]
            return jnp.concatenate([row[:, i : i + HEAD_DIM] for i in starts], 1)

        key = jnp.concatenate([key_ref[h], far_key_ref[h]], 0)
        value = jnp.concatenate([value_ref[h], far_value_ref[h]], 0)
        query = jnp.concatenate([ref[:, columns] for ref in query_refs], 0)
        grad = jnp.concatenate([part[:rows, columns] for part in parts], 0)
        scores = dot_nt(key, query) * scale
        attend = jnp.where(allowed, jnp.exp(scores - lanes(lse)), 0.0)
        score_grad = attend * (dot_nt(value, grad) - lanes(delta))
        value_part = dot(attend.astype(jnp.bfloat16), grad)
        key_part = dot(score_grad.astype(jnp.bfloat16), query)
        if last:
            key_in, value_in, own_ref, other_ref = refs
            key_part = (key_in[h] + key_part) * scale
            value_part = value_in[h] + value_part
            own_ref[0, h] = key_part[:rows].astype(jnp.bfloat16)
            own_ref[1, h] = value_part[:rows].astype(jnp.bfloat16)
            other_ref[0, h] = key_part[rows:].astype(jnp.bfloat16)
            other_ref[1, h] = value_part[rows:].astype(jnp.bfloat16)
        else:
            key_out, value_out = refs
            key_out[h] = key_part
            value_out[h] = value_part


def key_grads(
    ctx, key, value, far_key, far_value, every, query_pieces, queries, pieces, grads, sums
):
    heads = key.shape[0]
    n_ctx, _, rows = every.shape
    last = sums is not None
    each = 2
    width = each * HEAD_DIM
    places = FAR if last else NEAR
    counted = len(places) * rows
    mine = pl.BlockSpec((each, rows, HEAD_DIM), lambda h, ctx: (h, 0, 0))
    piece_specs = [
        pl.BlockSpec((piece.shape[0], width), lambda h, ctx: (0, h)) for piece in (*queries, *grads)
    ]
    sum_spec = pl.BlockSpec((each, 2 * rows, HEAD_DIM), lambda h, ctx: (h, 0, 0))
    pair_spec = pl.BlockSpec((2, each, rows, HEAD_DIM), lambda h, ctx: (0, h, 0, 0))
    sum_shape = (heads, 2 * rows, HEAD_DIM)
    pair_shape = (2, heads, rows, HEAD_DIM)
    here = [pltpu.VMEM((2 * rows, LANES), jnp.float32)]
    if last:
        extra_in = [sum_spec, sum_spec]
        out_specs = [pair_spec, pair_spec]
        out_shape = [jax.ShapeDtypeStruct(pair_shape, jnp.bfloat16)] * 2
    else:
        extra_in = []
        out_specs = [sum_spec, sum_spec]
        out_shape = [jax.ShapeDtypeStruct(sum_shape, jnp.float32)] * 2
    return pl.pallas_call(
        functools.partial(
            key_kernel, HEAD_DIM ** (-0.5), each, places, pieces, query_pieces, last
        ),
        grid_spec=pltpu.PrefetchScalarGridSpec(
            num_scalar_prefetch=1,
            grid=(heads // each,),
            in_specs=[mine] * 4
            + [
                pl.BlockSpec((n_ctx, 1, rows), lambda h, ctx: (0, 0, 0)),
            ]
            + piece_specs
            + extra_in,
            out_specs=out_specs,
            scratch_shapes=here,
        ),
        out_shape=out_shape,
        compiler_params=params(60),
        cost_estimate=pl.CostEstimate(
            flops=16 * rows * counted * heads * HEAD_DIM,
            bytes_accessed=8 * counted * heads * HEAD_DIM,
            transcendentals=2 * rows * counted * heads,
        ),
        name="key_grads_last" if last else "key_grads_first",
    )(ctx, key, value, far_key, far_value, every, *queries, *grads, *(sums or ()))


def finish_kernel(
    returned_ref, back_ref, hidden_ref, out_grad_ref, gain_ref, inverse_ref, along_ref, own_ref,
    arrived_ref, _, residual_ref, key_ref, value_ref,
):
    inverse = inverse_ref[:, :1]
    weighted = gain_ref[...] * dot(back_ref[...], returned_ref[...])
    hidden = hidden_ref[...].astype(jnp.float32)
    residual = out_grad_ref[...].astype(jnp.float32) + inverse * weighted
    residual = residual - hidden * (inverse * inverse * along_ref[:, :1])
    residual_ref[...] = residual.astype(jnp.bfloat16)
    for h in range(own_ref.shape[1]):
        columns = slice(h * HEAD_DIM, (h + 1) * HEAD_DIM)
        for i, out in enumerate((key_ref, value_ref)):
            total = own_ref[i, h].astype(jnp.float32) + arrived_ref[i, h].astype(jnp.float32)
            out[:, columns] = total.astype(jnp.bfloat16)


def finish(returned, back, hidden, out_grad, gain, inverse, along, own, arrived, residual):
    rows, model = hidden.shape
    slots, rest = returned.shape
    _, heads, _, size = own.shape
    whole = lambda shape: pl.BlockSpec(shape, lambda i: (0,) * len(shape))
    second = pl.BlockSpec((rows, rest), lambda i: (0, 1))
    flat = (rows, heads * size)
    return pl.pallas_call(
        finish_kernel,
        grid=(1,),
        in_specs=[
            whole((slots, rest)),
            whole((rows, slots)),
            second,
            second,
            pl.BlockSpec((1, rest), lambda i: (0, 1)),
            whole((rows, LANES)),
            whole((rows, LANES)),
            whole(own.shape),
            whole(own.shape),
            pl.BlockSpec(memory_space=pl.ANY),
        ],
        out_specs=[second, whole(flat), whole(flat)],
        out_shape=[
            jax.ShapeDtypeStruct((rows, model), jnp.bfloat16),
            jax.ShapeDtypeStruct(flat, jnp.bfloat16),
            jax.ShapeDtypeStruct(flat, jnp.bfloat16),
        ],
        input_output_aliases={9: 0},
        compiler_params=params(60),
        cost_estimate=pl.CostEstimate(
            flops=2 * slots * rows * rest, bytes_accessed=12 * rows * model, transcendentals=0
        ),
        name="finish",
    )(returned, back, hidden, out_grad, gain, inverse, along, own, arrived, residual)


def body(
    queries, keys, values, segments, hidden_state, norm_gain,
    route_gates, routes, out_grad, w_gate, w_up, w_down,
):
    rows, model = hidden_state.shape[1:]
    front = queries.shape[2]
    heads = front // HEAD_DIM
    n_exp = lax.axis_size("exp")
    capacity = 3 * rows * TOP // (2 * n_exp)
    hidden, grad_in = hidden_state[0], out_grad[0]
    gain = norm_gain[None, :]
    query, key, value = queries[0], keys[0], values[0]
    gate_mat, up_mat, down_mat = w_gate[0], w_up[0], w_down[0]
    n_ctx = lax.axis_size("ctx")
    ctx = lax.axis_index("ctx")[None]
    every = segments[0].reshape(n_ctx, 1, rows)

    def exchange(x):
        cut = x.reshape(n_exp, capacity, x.shape[1])
        return lax.all_to_all(cut, "exp", split_axis=0, concat_axis=0, tiled=True).reshape(x.shape)

    def right(x):
        return lax.ppermute(x, "ctx", [(i, (i + 4) % n_ctx) for i in range(n_ctx)])

    def left(x):
        return lax.ppermute(x, "ctx", [(i, (i - 4) % n_ctx) for i in range(n_ctx)])

    def across(x):
        return lax.ppermute(x, "ctx", [(i, i ^ 2) for i in range(n_ctx)])

    def swap_core(x):
        return lax.ppermute(x, "ctx", [(i, i ^ 1) for i in range(n_ctx)])

    def first_round(x):
        return across(x), right(x), left(x)

    def second_round(from_y, from_left, from_right):
        return right(from_left), left(from_y), across(from_left)

    def third_round(far, y_right, y_left):
        cut = far.shape[0] // 3
        return across(far[:cut]), left(y_right[cut : 2 * cut]), right(y_left[2 * cut :])

    send, back, inverse = pack(
        routes[0].T, route_gates[0].T, hidden, gain, grad_in, n_exp, capacity
    )
    def spread(x, near):
        half = x.shape[0] // 2
        from_y, from_left, from_right = near
        far = (right(from_left[:half]), left(from_right[half:]))
        return (x, *near, *far, left(from_y), right(from_y))

    def spread_last(parts):
        y_right, y_left = parts[-2:]
        half = y_right.shape[0] // 2
        return (*parts, right(y_left[:half]), left(y_right[half:]))

    pieces = (1, 1, 1, 1, 2, 1, 1, 2)
    key, value, query, inverse = lax.optimization_barrier((key, value, query, inverse))
    arrived = exchange(send)
    stacked = jnp.concatenate([key, value], 0)
    parts = spread(stacked, first_round(stacked))
    query_then, *parts = lax.optimization_barrier((query, *parts))
    blocks = spread_last(parts)
    other_blocks = [swap_core(block) for block in blocks]
    query_near = first_round(query_then)
    number = len(blocks)
    arrived, *all_blocks = lax.optimization_barrier(
        (arrived, *blocks, *other_blocks, *query_near)
    )
    blocks, other_blocks = all_blocks[:number], all_blocks[number : 2 * number]
    query_near = all_blocks[2 * number :]
    first, gate_grad, up_grad = expert(arrived, gate_mat, up_mat, down_mat, front)
    first = exchange(first)
    query, gate_grad = lax.optimization_barrier((query, gate_grad))
    query_parts = spread(query, query_near)
    second = second_rows(gate_grad, up_grad, gate_mat, up_mat, front)
    out, attend, lse_rows, *held = attend_own(
        ctx, query, every, pieces, blocks, other_blocks, heads
    )
    out, *query_parts = lax.optimization_barrier((out, *query_parts))
    query_parts = spread_last(query_parts)
    first, second, *query_parts = lax.optimization_barrier((first, second, *query_parts))
    grad, delta, along, residual = front_grad(
        first, back, hidden, grad_in, gain, inverse, out, lse_rows, heads
    )
    near = first_round(grad)
    half = heads // 2
    query_front = query_grads(grad, attend, *held, delta, 0, half, ())
    grad_then, query_front, *near = lax.optimization_barrier((grad, query_front, *near))
    far = second_round(*near)
    query_grad = query_grads(
        grad_then, attend, *held, delta, half, half, (query_front,)
    )
    held_back = lax.optimization_barrier((second, query_grad, *far, grad_then, *near))
    second, query_grad, far, near = held_back[0], held_back[1], held_back[2:5], held_back[5:]
    second = exchange(second)
    last = third_round(*far)
    sums = key_grads(
        ctx, *held, every, (1,) * 4, query_parts[:4], (1,) * 4, tuple(near), None
    )
    own, other = key_grads(
        ctx, *held, every, (2, 1, 1, 2), query_parts[4:], (1, 1, 1, 3), (*far, *last), sums
    )
    residual_grad, key_grad, value_grad = finish(
        second, back, hidden, grad_in, gain, inverse, along, own, swap_core(other), residual
    )
    return (query_grad[None], key_grad[None], value_grad[None], residual_grad[None])


def solution(mesh):
    rows = P("exp", "ctx", None)
    mats = P("exp", None, None)
    in_specs = (rows, rows, rows, P("exp", None), rows, P(), rows, rows, rows, mats, mats, mats)
    return jax.shard_map(
        body, mesh=mesh, in_specs=in_specs, out_specs=(rows,) * 4, check_vma=False
    )
```
